256 devices in a mesh: freq: 2 (over x_lo), row: 8 (over y, core), col: 16 (over x_hi, z).
Axes of the slice: x: 4 (x_hi: 2, x_lo: 2; x = x_hi * 2 + x_lo), y: 4, z: 8, core: 2. Of those that a mesh axis runs over, the one named last changes fastest.
Arguments:
- tiles: bfloat16 [256, 512, 512], P('col'), may hold values from -0.125 to 0.125
- tile_blocks: int32 [256, 1], P('col'), may hold values from 0 to 15; in each aligned block of 16 rows (0 to 15, 16 to 31, ...) at most 2 rows name the same one
- tile_pairs: int32 [256], P('col'), may hold values from 0 to 3
- tile_counts: int32 [16], P('col'), may hold values from 1 to 16, 224 in all
- left_panel: bfloat16 [8192, 2048], P('row'), may hold values from -6 to 6
- gaps: float32 [2048], replicated, may hold values from 0.05 to 2
- times: float32 [4], replicated, may hold values from 0.2 to 3
- cos_weights: float32 [4, 4], replicated, may hold values from -4 to 4
- bank: bfloat16 [8192, 1024], P('col', 'row'), may hold values from -0.0625 to 0.0625
- probe_idx: int32 [512], replicated, may hold values from 0 to 1023
Outputs:
- response: float32 [4, 8192, 512], P('freq', 'row', 'col')
The draws below stay inside these ranges and needn't reach their ends.
Inputs may be any that keep to these rules, and one draw needn't show every extreme that they name: `tile_blocks`: among the 16 listed tiles of one index of col no auxiliary block appears more than 2 times, and on some index of col some block appears exactly 2 times. `tile_counts`: the live tiles of an index of col are its first ones; some index has all 16 live.
All inputs are finite; a program needn't handle non-finite values. No bound on the sum of `tile_counts` on one device may be relied on, other than what follows from the above.
Results may differ from the reference program's by a relative error of at most 0.0065.
Values may be sent and summed in bfloat16 or wider, within the bound.
No kernel may reach another device: no remote copies, remote signals or barrier semaphores. Data moves between devices by JAX's collectives and lax.ppermute only.
A program may use at most 128 MiB of HBM per device.

```python
import math
import jax
import jax.numpy as jnp
import numpy as np
from jax import lax

NAUX = 8192
TILE = 512
MB = 4
NT = 4
NF = 4
SLOTS = 16
CAP = 2
NBANK = 1024
NPROBE = 512
NPAIR = 2048
NB = 16
LISTED = 256
N_COL = 16


def touch_ends(drawn, key, low, top_value):
    index_at = [jax.random.randint(jax.random.fold_in(key, axis), (), 0, length) for axis, length in enumerate(drawn.shape)]
    main_axis = drawn.shape.index(max(drawn.shape))
    beside = index_at[:main_axis] + [(index_at[main_axis] + 1) % drawn.shape[main_axis]] + index_at[main_axis + 1:]
    return drawn.at[tuple(index_at)].set(low).at[tuple(beside)].set(top_value)


def level_of(own_key, shape, cuts, low, top_value):
    loudness = 1.0
    for axis_at, parts in cuts:
        heights = jax.random.uniform(jax.random.fold_in(jax.random.fold_in(own_key, 6), axis_at), (parts,), jnp.float32, low / len(cuts), top_value / len(cuts))
        loudness = loudness * jnp.repeat(jnp.exp(heights), shape[axis_at] // parts).reshape((-1,) + (1,) * (len(shape) - 1 - axis_at))
    return loudness


def length_profile(number_of, total, most, skew):
    loads = [(1 << 20) // math.isqrt(standing ** skew) + 1 for standing in range(2, number_of + 1)]
    rest, holding = total - most - (number_of - 1), [1] * (number_of - 1)
    while rest > 0:
        movable = [i for i in range(number_of - 1) if holding[i] < most]
        mass, budget = sum([loads[i] for i in movable]), rest
        for i in movable:
            addition = min(most - holding[i], max(1, budget * loads[i] // mass), rest)
            holding[i] = holding[i] + addition
            rest = rest - addition
    return np.array([most] + holding)


def uneven(key, number_of, total, reach, lean):
    if number_of == 2:
        one = jax.random.randint(key, (), max(1, total - reach), min(reach, total - 1) + 1)
        return jnp.stack([one, total - one])
    lengths = jnp.asarray(length_profile(number_of, total, reach, lean), jnp.int32)
    pairs = (number_of - 1) // 2
    giver, sink = lengths[1:1 + 2 * pairs:2], lengths[2:2 + 2 * pairs:2]
    margin = jnp.minimum(giver - 1, reach - sink)
    moved = jax.random.randint(jax.random.fold_in(key, 1), (pairs,), 0, 1 << 20) % (margin + 1)
    lengths = lengths.at[1:1 + 2 * pairs:2].set(giver - moved).at[2:2 + 2 * pairs:2].set(sink + moved)
    return lengths[jax.random.permutation(jax.random.fold_in(key, 2), number_of)]


def deal_out(key, own, number, rows, amount, top, reach, skew):
    sequence = jax.random.permutation(key, amount)
    crowded, common = shares(amount, rows * top, reach, skew, True), shares(amount, rows * top, reach, skew, False)
    places = jnp.arange(amount)

    def named(tallies, rotation):
        used = int((tallies > 0).sum())
        fixed = max(1, used // 4)
        moved = fixed + (places - fixed + rotation * (used - fixed)) % max(1, amount - fixed)
        return jnp.zeros((amount,), jnp.int32).at[sequence[jnp.where(places < fixed, places, moved)]].set(jnp.asarray(tallies, jnp.int32))

    tallies = jnp.where(number % 4 == 0, named(crowded, number // 4), named(common, number - number // 4 - 1))
    mixed = jax.random.permutation(jax.random.fold_in(own, 3), amount)
    giver, sink = mixed[0:amount // 2 * 2:2], mixed[1:amount // 2 * 2:2]
    slack = jnp.minimum(tallies[giver] - 1, reach - tallies[sink]) // 2
    slack = jnp.where((giver == sequence[0]) | (sink == sequence[0]) | (tallies[sink] == 0), 0, jnp.maximum(slack, 0))
    moved = jax.random.randint(jax.random.fold_in(own, 4), (amount // 2,), 0, 1 << 20) % (slack + 1)
    tallies = tallies.at[giver].add(-moved).at[sink].add(moved)
    items = jnp.searchsorted(jnp.cumsum(tallies), jnp.arange(rows * top), side="right").astype(jnp.int32)
    listing = items.reshape(top, rows).T
    listing = listing[jax.random.permutation(jax.random.fold_in(own, 1), rows)]
    rotation = jax.random.randint(jax.random.fold_in(own, 2), (rows, 1), 0, top)
    return jnp.take_along_axis(listing, (jnp.arange(top)[None, :] + rotation) % top, axis=1)


def shares(count, total, bound, slope, full):
    weights = [(1 << 20) // math.isqrt(rank ** slope) + 1 for rank in range(1, count + 1)]
    largest = bound if full else min(bound, max(-(-total // count), total * weights[0] // sum(weights)))
    least = 1 if total - largest >= count - 1 else 0
    counts, spare = [largest] + [least] * (count - 1), total - largest - least * (count - 1)
    while spare > 0:
        candidates = [i for i in range(1, count) if counts[i] < largest] or [i for i in range(1, count) if counts[i] < bound]
        whole, budget = sum([weights[i] for i in candidates]), spare
        for i in candidates:
            more = min(bound - counts[i], max(1, budget * weights[i] // whole), spare)
            counts[i] = counts[i] + more
            spare = spare - more
    return np.array(counts)


def bell_draw(key, shape, scale, limit, split=(), kind=jnp.bfloat16):
    entries = jax.random.normal(key, shape, jnp.float32) * scale
    if len(split) > 0:
        entries = level_of(key, shape, split, -0.22, 0.18) * entries
    return jnp.clip(entries, min=-limit, max=limit).astype(kind)


def setup_inputs(seed: int = 0) -> dict:
    keys = jax.random.split(jax.random.key(seed), 11)
    tiles = bell_draw(keys[0], (LISTED, TILE, TILE), NPAIR ** -0.5, 0.125, ((0, 16),))
    tile_blocks_keys = jax.random.split(jax.random.fold_in(keys[1], 1), LISTED // SLOTS)
    tile_blocks_turns = jax.random.permutation(jax.random.fold_in(keys[1], 3), LISTED // SLOTS)
    tile_blocks = jax.vmap(lambda own, number: deal_out(jax.random.fold_in(keys[1], 2), own, number, SLOTS, NB, 1, CAP, 1))(tile_blocks_keys, tile_blocks_turns).reshape((LISTED, 1))
    tile_pairs = touch_ends(jax.random.randint(keys[2], (LISTED,), 0, MB), jax.random.fold_in(keys[2], 1), 0, MB - 1).astype(jnp.int32)
    tile_counts = uneven(keys[3], N_COL, N_COL * SLOTS * 7 // 8, SLOTS, 1).astype(jnp.int32)
    left_panel = bell_draw(keys[4], (NAUX, NPAIR), 1.0, 6.0, ((0, 8),))
    gaps = jnp.clip(jnp.exp(jax.random.uniform(keys[5], (NPAIR,), jnp.float32, math.log(0.05), math.log(2.0))), 0.05, 2.0)
    times = jnp.clip(jnp.exp(jax.random.uniform(keys[6], (NT,), jnp.float32, math.log(0.2), math.log(3.0))), 0.2, 3.0)
    cos_weights = bell_draw(keys[7], (NF, NT), 1.0, 4.0, (), jnp.float32)
    bank = bell_draw(keys[8], (NAUX, NBANK), NAUX ** -0.5, 0.0625, ((0, 16), (1, 8)))
    probe_idx = touch_ends(jax.random.randint(keys[9], (NPROBE,), 0, NBANK), jax.random.fold_in(keys[9], 1), 0, NBANK - 1).astype(jnp.int32)
    return dict(tiles=tiles, tile_blocks=tile_blocks, tile_pairs=tile_pairs, tile_counts=tile_counts, left_panel=left_panel, gaps=gaps, times=times, cos_weights=cos_weights, bank=bank, probe_idx=probe_idx)


def reference(tiles, tile_blocks, tile_pairs, tile_counts, left_panel, gaps, times, cos_weights, bank, probe_idx):
    listed = tiles.shape[0]
    slot_count = listed // N_COL
    block_total = NAUX // TILE
    positions = jnp.arange(listed, dtype=jnp.int32)
    alive_slot = (positions % slot_count) < jnp.repeat(tile_counts, slot_count)
    weights = jnp.where(alive_slot, 1.0, 0.0).astype(jnp.float32)
    assembled = jnp.zeros((block_total, MB, TILE, TILE), jnp.float32)
    assembled = assembled.at[tile_blocks[:, 0], tile_pairs].add(tiles.astype(jnp.float32) * weights[:, None, None])
    assembled = assembled.transpose(0, 2, 1, 3).reshape(NAUX, NPAIR)
    probes = jnp.take(bank, probe_idx, axis=1).astype(jnp.float32)
    decays = jnp.exp(-gaps[None, :] * times[:, None])

    def one_block(carry, block_index):
        start = (block_index * TILE).astype(jnp.int32)
        slab = lax.dynamic_slice_in_dim(assembled, start, TILE, 0)
        probe_rows = lax.dynamic_slice_in_dim(probes, start, TILE, 0)
        pieces = []
        for which in range(NT):
            scaled = (slab * decays[which][None, :]).astype(jnp.bfloat16)
            pieces.append(jnp.dot(left_panel, scaled.T, preferred_element_type=jnp.float32))
        stacked = jnp.stack(pieces)
        screened = jnp.einsum("fk,kij->fij", cos_weights, stacked, precision=lax.Precision.HIGHEST)
        added = jnp.einsum("fij,jp->fip", screened, probe_rows, precision=lax.Precision.HIGHEST)
        return carry + added, None

    start_value = jnp.zeros((NF, NAUX, NPROBE), jnp.float32)
    result, unused = lax.scan(one_block, start_value, jnp.arange(block_total, dtype=jnp.int32))
    return result
```

```python
import jax
import jax.numpy as jnp
from jax import lax
from jax.experimental import pallas as pl
from jax.experimental.pallas import tpu as pltpu
from jax.sharding import Mesh, PartitionSpec as P

TILE = 512
HALF = 256
MB = 4
SLOTS = 16
NB = 16
NPAIR = 2048
SET = 32
BANKED = 128
F32 = jnp.float32
BF16 = jnp.bfloat16


def gather_probes(banked, probe_idx):
    def kernel(bank_ref, idx_ref, own_ref, send_ref):
        core = lax.axis_index("k")
        which = lax.axis_index("f") * 4 + lax.axis_index("y")
        wanted = idx_ref[pl.ds(which, 1), :]
        picks = []
        for y in range(4):
            here = lax.broadcasted_iota(jnp.int32, (BANKED, 2 * SET), 0) + (y * 2 + core) * BANKED
            picks.append(jnp.where(here == wanted, 1.0, 0.0).T.astype(BF16))
        for out_ref, at in ((own_ref, core), (send_ref, 1 - core)):
            rows = pl.ds(pl.multiple_of(at * HALF, HALF), HALF)
            total = jnp.zeros((2 * SET, HALF), F32)
            for y in range(4):
                total += lax.dot_general(
                    picks[y], bank_ref[y, rows, :], (((1,), (1,)), ((), ())), preferred_element_type=F32
                )
            out_ref[...] = total.astype(BF16)

    shape = jax.ShapeDtypeStruct((2 * SET, HALF), BF16)
    return pl.pallas_call(kernel, out_shape=(shape, shape), name="gather_probes")(banked, probe_idx)


def tile_products(tiles, blocks, pairs, counts, probes):
    def kernel(blocks_ref, pairs_ref, counts_ref, tiles_ref, probes_ref, own_ref, send_ref, held, total, sems):
        core = lax.axis_index("k")
        rows = pl.ds(pl.multiple_of(core * HALF, HALF), HALF)
        live = counts_ref[0]

        def copy(s):
            return pltpu.make_async_copy(tiles_ref.at[s, rows, :], held.at[s], sems.at[s])

        for s in range(SLOTS):
            @pl.when(s < live)
            def _():
                copy(s).start()

        total[...] = jnp.zeros_like(total)
        for s in range(SLOTS):
            @pl.when(s < live)
            def _():
                copy(s).wait()
                at = pairs_ref[s]
                total[at] += jnp.dot(probes_ref[blocks_ref[s]], held[s], preferred_element_type=F32)

        mine = pl.ds(pl.multiple_of(core * SET, SET), SET)
        theirs = pl.ds(pl.multiple_of((1 - core) * SET, SET), SET)
        for at in range(MB):
            columns = pl.ds(at * TILE, TILE)
            own_ref[:, columns] = total[at, mine, :]
            send_ref[:, columns] = total[at, theirs, :].astype(BF16)

    smem = pl.BlockSpec(memory_space=pltpu.SMEM)
    vmem = pl.BlockSpec(memory_space=pltpu.VMEM)
    return pl.pallas_call(
        kernel,
        out_shape=(jax.ShapeDtypeStruct((SET, NPAIR), F32), jax.ShapeDtypeStruct((SET, NPAIR), BF16)),
        in_specs=[smem, smem, smem, pl.BlockSpec(memory_space=pl.ANY), vmem],
        out_specs=(vmem, vmem),
        scratch_shapes=[
            pltpu.VMEM((SLOTS, HALF, TILE), BF16),
            pltpu.VMEM((MB, 2 * SET, TILE), F32),
            pltpu.SemaphoreType.DMA((SLOTS,)),
        ],
        compiler_params=pltpu.CompilerParams(vmem_limit_bytes=16 << 20),
        name="tile_products",
    )(blocks, pairs, counts, tiles, probes)


def screened_response(partials, left_panel, gaps, times, cos_weights):
    terms = partials.shape[0]
    rows = left_panel.shape[0]
    block = 256

    def kernel(times_ref, cos_ref, partials_ref, gaps_ref, left_ref, out_ref, scaled):
        @pl.when(pl.program_id(0) == 0)
        def _():
            first = lax.axis_index("f") * 2
            whole = partials_ref[0].astype(F32)
            for n in range(1, terms):
                whole += partials_ref[n].astype(F32)
            decays = [jnp.exp(-gaps_ref[...] * times_ref[k]) for k in range(4)]
            for f in range(2):
                weight = decays[0] * cos_ref[first + f, 0]
                for k in range(1, 4):
                    weight += decays[k] * cos_ref[first + f, k]
                scaled[f * SET : (f + 1) * SET, :] = (whole * weight).astype(BF16)

        product = lax.dot_general(
            left_ref[...], scaled[...], (((1,), (1,)), ((), ())), preferred_element_type=F32
        )
        out_ref[0] = product[:, :SET]
        out_ref[1] = product[:, SET:]

    smem = pl.BlockSpec(memory_space=pltpu.SMEM)
    return pl.pallas_call(
        kernel,
        grid=(rows // block,),
        out_shape=jax.ShapeDtypeStruct((2, rows, SET), F32),
        in_specs=[
            smem,
            smem,
            pl.BlockSpec((terms, SET, NPAIR), lambda i: (0, 0, 0)),
            pl.BlockSpec((1, NPAIR), lambda i: (0, 0)),
            pl.BlockSpec((block, NPAIR), lambda i: (i, 0)),
        ],
        out_specs=pl.BlockSpec((2, block, SET), lambda i: (0, i, 0)),
        scratch_shapes=[pltpu.VMEM((2 * SET, NPAIR), BF16)],
        compiler_params=pltpu.CompilerParams(vmem_limit_bytes=16 << 20),
        name="screened_response",
    )(times, cos_weights, partials, gaps, left_panel)


def summed(parts):
    return jnp.sum(parts.astype(F32), axis=0).astype(BF16)


def shards(
    tiles, tile_blocks, tile_pairs, tile_counts, left_panel, gaps, times, cos_weights, bank, probe_idx
):
    swap = [(0, 1), (1, 0)]
    with jax.named_scope("probes"):
        banked = lax.all_gather(bank, "y", axis=0)
        kept, sent = gather_probes(banked, probe_idx.reshape(8, 2 * SET))
        probes = kept + lax.ppermute(sent, "k", swap)
        probes = lax.all_gather(probes, "z", axis=0)
        probes = lax.all_gather(probes, "u", axis=0).reshape(NB, 2 * SET, HALF)
    with jax.named_scope("products"):
        kept, sent = tile_products(tiles, tile_blocks.reshape(SLOTS), tile_pairs, tile_counts, probes)
        partial = (kept + lax.ppermute(sent, "k", swap).astype(F32)).astype(BF16)
    with jax.named_scope("exchange"):
        turned = [(a * 16 + c, c * 16 + a) for a in range(16) for c in range(16)]
        partial = lax.ppermute(partial, ("f", "y", "k", "u", "z"), turned)
        partial = summed(lax.all_gather(partial, "k", axis=0))
        partial = summed(lax.all_gather(partial, "y", axis=0))
        partials = lax.all_gather(partial, "f", axis=0)
    with jax.named_scope("response"):
        return screened_response(partials, left_panel, gaps.reshape(1, NPAIR), times, cos_weights)


def solution(mesh):
    fine = Mesh(mesh.devices.reshape(2, 4, 2, 2, 8), ("f", "y", "k", "u", "z"))
    row, col = ("y", "k"), ("u", "z")
    placed = (
        P(col, None, None),
        P(col, None),
        P(col),
        P(col),
        P(row, None),
        P(),
        P(),
        P(),
        P(col, row),
        P(),
    )
    return jax.shard_map(
        shards, mesh=fine, in_specs=placed, out_specs=P("f", row, col), check_vma=False
    )
```

```python
import jax
import jax.numpy as jnp
from jax import lax
from jax.experimental import pallas as pl
from jax.experimental.pallas import tpu as pltpu
from jax.sharding import Mesh, PartitionSpec as P

TILE = 512
MB = 4
CAP = 2
SLOTS = 16
NB = 16
NPAIR = 2048
NPROBE = 512
SET = 32
PART = 32
CODE = 16
ROWS = CAP * PART + CODE
LANES = 128
F32 = jnp.float32
BF16 = jnp.bfloat16
SMEM = pl.BlockSpec(memory_space=pltpu.SMEM)
VMEM = pl.BlockSpec(memory_space=pltpu.VMEM)


def place():
    return lax.axis_index("f") * 8 + lax.axis_index("y") * 2 + lax.axis_index("k")


def outgoing_parts(tiles, blocks, pairs, counts):
    def kernel(blocks_ref, pairs_ref, counts_ref, tiles_ref, out_ref, held, sems):
        me = place()
        lanes = pl.ds(pl.multiple_of(me // 4 * LANES, LANES), LANES)
        live = counts_ref[0]

        def copy(s):
            return pltpu.make_async_copy(tiles_ref.at[s, :, lanes], held.at[s], sems.at[s])

        for s in range(SLOTS):
            @pl.when(s < live)
            def _():
                copy(s).start()

        out_ref[...] = jnp.zeros_like(out_ref)
        wanted = lax.broadcasted_iota(jnp.int32, (PART, LANES), 0) + me % 4 * PART
        pick = jnp.where(wanted == lax.broadcasted_iota(jnp.int32, (PART, LANES), 1), 1.0, 0.0).astype(BF16)
        second = lax.broadcasted_iota(jnp.int32, (CODE, TILE), 0) // (CODE // CAP)
        for s in range(SLOTS):
            @pl.when(s < live)
            def _():
                owner = blocks_ref[s]
                earlier = jnp.int32(0)
                for t in range(s):
                    earlier += jnp.where(blocks_ref[t] == owner, 1, 0)
                copy(s).wait()
                part = lax.dot_general(pick, held[s], (((1,), (1,)), ((), ())), preferred_element_type=F32)
                out_ref[owner, pl.ds(pl.multiple_of(earlier * PART, PART), PART), :] = part.astype(BF16)
                codes = out_ref[owner, CAP * PART :, :].astype(F32)
                codes = jnp.where(second == earlier, pairs_ref[s].astype(F32), codes)
                out_ref[owner, CAP * PART :, :] = codes.astype(BF16)

    return pl.pallas_call(
        kernel,
        out_shape=jax.ShapeDtypeStruct((NB, ROWS, TILE), BF16),
        in_specs=[SMEM, SMEM, SMEM, pl.BlockSpec(memory_space=pl.ANY)],
        out_specs=VMEM,
        scratch_shapes=[pltpu.VMEM((SLOTS, TILE, LANES), BF16), pltpu.SemaphoreType.DMA((SLOTS,))],
        compiler_params=pltpu.CompilerParams(vmem_limit_bytes=56 << 20),
        name="outgoing_parts",
    )(blocks, pairs, counts, tiles)


def picked_probes(own, other, probe_idx):
    def kernel(own_ref, other_ref, idx_ref, out_ref):
        core = lax.axis_index("k")
        total = jnp.zeros((TILE, NPROBE), F32)
        for bank_ref, at in ((own_ref, core), (other_ref, 1 - core)):
            for y in range(4):
                here = lax.broadcasted_iota(jnp.int32, (LANES, NPROBE), 0) + (y * 2 + at) * LANES
                pick = jnp.where(here == idx_ref[...], 1.0, 0.0).astype(BF16)
                total += jnp.dot(bank_ref[y], pick, preferred_element_type=F32)
        out_ref[...] = total.astype(BF16)

    return pl.pallas_call(
        kernel,
        out_shape=jax.ShapeDtypeStruct((TILE, NPROBE), BF16),
        compiler_params=pltpu.CompilerParams(vmem_limit_bytes=16 << 20),
        name="picked_probes",
    )(own, other, probe_idx)


def owner_products(parts, probes):
    def kernel(parts_ref, probes_ref, out_ref, product):
        rows = parts_ref[:, : CAP * PART, :].reshape(NB * CAP * PART, TILE)
        product[...] = jnp.dot(rows, probes_ref[...], preferred_element_type=F32)
        for m in range(MB):
            total = jnp.zeros((PART, NPROBE), F32)
            for c in range(NB):
                for j in range(CAP):
                    code = parts_ref[c, CAP * PART :, :].astype(F32)[j * (CODE // CAP) : j * (CODE // CAP) + 1, :]
                    start = (c * CAP + j) * PART
                    total += jnp.where(code == m, product[start : start + PART, :], 0.0)
            turned = total.T.astype(BF16)
            for c in range(NB):
                out_ref[c, :, m * PART : (m + 1) * PART] = turned[c * SET : (c + 1) * SET, :]

    return pl.pallas_call(
        kernel,
        out_shape=jax.ShapeDtypeStruct((NB, SET, MB * PART), BF16),
        scratch_shapes=[pltpu.VMEM((NB * CAP * PART, NPROBE), F32)],
        compiler_params=pltpu.CompilerParams(vmem_limit_bytes=16 << 20),
        name="owner_products",
    )(parts, probes)


def screened_response(parts, left_panel, gaps, times, cos_weights):
    rows = left_panel.shape[0]
    block = 256

    def kernel(times_ref, cos_ref, parts_ref, gaps_ref, left_ref, out_ref, scaled):
        @pl.when(pl.program_id(0) == 0)
        def _():
            first = lax.axis_index("f") * 2
            lane = lax.broadcasted_iota(jnp.int32, (SET, LANES), 1) // PART
            decays = [jnp.exp(-gaps_ref[...] * times_ref[k]) for k in range(4)]
            weights = []
            for f in range(2):
                weight = decays[0] * cos_ref[first + f, 0]
                for k in range(1, 4):
                    weight += decays[k] * cos_ref[first + f, k]
                weights.append(weight)
            for g in range(4):
                held = [parts_ref[(4 * g + sub) // 2, sub % 2].astype(F32) for sub in range(4)]
                for m in range(MB):
                    whole = held[m]
                    for sub in range(4):
                        if sub != m:
                            whole = jnp.where(lane == sub, pltpu.roll(held[sub], (sub - m) % 4 * PART, 1), whole)
                    at = (m * 4 + g) * LANES
                    for f in range(2):
                        scaled[f * SET : (f + 1) * SET, at : at + LANES] = (
                            whole * weights[f][:, at : at + LANES]
                        ).astype(BF16)

        product = lax.dot_general(
            scaled[...], left_ref[...], (((1,), (1,)), ((), ())), preferred_element_type=F32
        )
        out_ref[0] = product[:SET]
        out_ref[1] = product[SET:]

    return pl.pallas_call(
        kernel,
        grid=(rows // block,),
        out_shape=jax.ShapeDtypeStruct((2, SET, rows), F32),
        in_specs=[
            SMEM,
            SMEM,
            pl.BlockSpec((8, 2, SET, LANES), lambda i: (0, 0, 0, 0)),
            pl.BlockSpec((1, NPAIR), lambda i: (0, 0)),
            pl.BlockSpec((block, NPAIR), lambda i: (i, 0)),
        ],
        out_specs=pl.BlockSpec((2, SET, block), lambda i: (0, 0, i)),
        scratch_shapes=[pltpu.VMEM((2 * SET, NPAIR), BF16)],
        compiler_params=pltpu.CompilerParams(vmem_limit_bytes=56 << 20),
        name="screened_response",
    )(times, cos_weights, parts, gaps, left_panel)


def shards(
    tiles, tile_blocks, tile_pairs, tile_counts, left_panel, gaps, times, cos_weights, bank, probe_idx
):
    with jax.named_scope("parts"):
        parts = outgoing_parts(tiles, tile_blocks.reshape(SLOTS), tile_pairs, tile_counts)
        parts = lax.all_to_all(parts, ("u", "z"), 0, 0, tiled=True)
    with jax.named_scope("probes"):
        banked = lax.all_gather(bank, "y", axis=0)
        probes = picked_probes(banked, lax.ppermute(banked, "k", [(0, 1), (1, 0)]), probe_idx.reshape(1, NPROBE))
    with jax.named_scope("products"):
        products = owner_products(parts, probes)
        products = lax.all_to_all(products, ("u", "z"), 0, 0, tiled=True)
        product = jnp.sum(products.astype(F32), axis=0).astype(BF16)
    with jax.named_scope("spread"):
        both = lax.all_gather(product, "k", axis=0)
        both = lax.all_to_all(jnp.broadcast_to(both, (8,) + both.shape), ("f", "y"), 0, 0, tiled=True)
    with jax.named_scope("response"):
        turned = screened_response(both, left_panel, gaps.reshape(1, NPAIR), times, cos_weights)
        return jnp.swapaxes(turned, 1, 2)


def solution(mesh):
    fine = Mesh(mesh.devices.reshape(2, 4, 2, 2, 8), ("f", "y", "k", "u", "z"))
    row, col = ("y", "k"), ("u", "z")
    placed = (
        P(col, None, None),
        P(col, None),
        P(col),
        P(col),
        P(row, None),
        P(),
        P(),
        P(),
        P(col, row),
        P(),
    )
    return jax.shard_map(
        shards, mesh=fine, in_specs=placed, out_specs=P("f", row, col), check_vma=False
    )
```

```python
import jax
import jax.numpy as jnp
from jax import lax
from jax.experimental import pallas as pl
from jax.experimental.pallas import tpu as pltpu
from jax.sharding import Mesh, PartitionSpec as P

TILE = 512
MB = 4
CAP = 2
SLOTS = 16
NB = 16
NPAIR = 2048
NPROBE = 512
SET = 32
PART = 32
CODE = 16
LANES = 128
CHUNKS = 4
UNIT = PART * TILE // LANES
ROWS = CAP * UNIT + CODE
F32 = jnp.float32
BF16 = jnp.bfloat16
SMEM = pl.BlockSpec(memory_space=pltpu.SMEM)
VMEM = pl.BlockSpec(memory_space=pltpu.VMEM)


def place():
    return lax.axis_index("f") * 8 + lax.axis_index("y") * 2 + lax.axis_index("k")


def outgoing_parts(tiles, blocks, pairs, counts):
    def kernel(blocks_ref, pairs_ref, counts_ref, tiles_ref, out_ref, held, parts, source, sems):
        me = place()
        lanes = pl.ds(pl.multiple_of(me // 4 * LANES, LANES), LANES)

        def copy(s):
            return pltpu.make_async_copy(tiles_ref.at[s, :, lanes], held.at[s], sems.at[s])

        for s in range(SLOTS):
            copy(s).start()
        live = counts_ref[0]
        for d in range(NB * CAP):
            source[d] = -1
        for s in range(SLOTS):
            at = blocks_ref[s] * CAP
            at = jnp.where(source[at] >= 0, at + 1, at)
            source[at] = jnp.where(s < live, s, source[at])

        wanted = lax.broadcasted_iota(jnp.int32, (PART, LANES), 0) + me % 4 * PART
        pick = jnp.where(wanted == lax.broadcasted_iota(jnp.int32, (PART, LANES), 1), 1.0, 0.0).astype(BF16)
        for s in range(SLOTS):
            copy(s).wait()
            part = lax.dot_general(pick, held[s], (((1,), (1,)), ((), ())), preferred_element_type=F32)
            for n in range(TILE // LANES):
                parts[s, n * PART : (n + 1) * PART, :] = part[:, n * LANES : (n + 1) * LANES].astype(BF16)

        second = lax.broadcasted_iota(jnp.int32, (CODE, LANES), 0) >= CODE // CAP
        for d in range(NB):
            codes = []
            for j in range(CAP):
                s = source[d * CAP + j]
                there = jnp.maximum(s, 0)
                full = jnp.where(s >= 0, 1.0, 0.0).astype(BF16)
                out_ref[d, j * UNIT : (j + 1) * UNIT, :] = parts[there] * full
                codes.append(pairs_ref[there].astype(F32))
            out_ref[d, CAP * UNIT :, :] = jnp.where(second, codes[1], codes[0]).astype(BF16)

    return pl.pallas_call(
        kernel,
        out_shape=jax.ShapeDtypeStruct((NB, ROWS, LANES), BF16),
        in_specs=[SMEM, SMEM, SMEM, pl.BlockSpec(memory_space=pl.ANY)],
        out_specs=VMEM,
        scratch_shapes=[
            pltpu.VMEM((SLOTS, TILE, LANES), BF16),
            pltpu.VMEM((SLOTS, UNIT, LANES), BF16),
            pltpu.SMEM((NB * CAP,), jnp.int32),
            pltpu.SemaphoreType.DMA((SLOTS,)),
        ],
        compiler_params=pltpu.CompilerParams(vmem_limit_bytes=56 << 20),
        name="outgoing_parts",
    )(blocks, pairs, counts, tiles)


def picked_probes(own, other, probe_idx, gaps, times, cos_weights):
    def kernel(times_ref, cos_ref, own_ref, other_ref, idx_ref, gaps_ref, out_ref, weights_ref):
        core = lax.axis_index("k")
        total = jnp.zeros((TILE, NPROBE), F32)
        for bank_ref, at in ((own_ref, core), (other_ref, 1 - core)):
            for y in range(4):
                here = lax.broadcasted_iota(jnp.int32, (LANES, NPROBE), 0) + (y * 2 + at) * LANES
                pick = jnp.where(here == idx_ref[...], 1.0, 0.0).astype(BF16)
                total += jnp.dot(bank_ref[y], pick, preferred_element_type=F32)
        out_ref[...] = total.astype(BF16)
        first = lax.axis_index("f") * 2
        decays = [jnp.exp(-gaps_ref[...] * times_ref[k]) for k in range(4)]
        for f in range(2):
            weight = decays[0] * cos_ref[first + f, 0]
            for k in range(1, 4):
                weight += decays[k] * cos_ref[first + f, k]
            weights_ref[f : f + 1, :] = weight

    return pl.pallas_call(
        kernel,
        out_shape=(jax.ShapeDtypeStruct((TILE, NPROBE), BF16), jax.ShapeDtypeStruct((2, NPAIR), F32)),
        in_specs=[SMEM, SMEM, VMEM, VMEM, VMEM, VMEM],
        out_specs=(VMEM, VMEM),
        compiler_params=pltpu.CompilerParams(vmem_limit_bytes=24 << 20),
        name="picked_probes",
    )(times, cos_weights, own, other, probe_idx, gaps)


def owner_products(parts, probes):
    def kernel(parts_ref, probes_ref, out_ref, product):
        units = parts_ref[:, : CAP * UNIT, :].reshape(NB * CAP, TILE // LANES, PART, LANES)
        rows = jnp.concatenate([units[:, n] for n in range(TILE // LANES)], axis=-1).reshape(NB * CAP * PART, TILE)
        product[...] = jnp.dot(rows, probes_ref[...], preferred_element_type=F32)
        codes = [
            parts_ref[c, CAP * UNIT :, :].astype(F32)[j * (CODE // CAP) : j * (CODE // CAP) + 1, :1]
            for c in range(NB)
            for j in range(CAP)
        ]
        for m in range(MB):
            total = jnp.zeros((PART, NPROBE), F32)
            for n, code in enumerate(codes):
                total += jnp.where(code == m, product[n * PART : (n + 1) * PART, :], 0.0)
            turned = total.T.astype(BF16)
            for c in range(NB):
                out_ref[c, :, m * PART : (m + 1) * PART] = turned[c * SET : (c + 1) * SET, :]

    return pl.pallas_call(
        kernel,
        out_shape=jax.ShapeDtypeStruct((NB, SET, MB * PART), BF16),
        scratch_shapes=[pltpu.VMEM((NB * CAP * PART, NPROBE), F32)],
        compiler_params=pltpu.CompilerParams(vmem_limit_bytes=16 << 20),
        name="owner_products",
    )(parts, probes)


def screened_response(parts, left_panel, weights):
    rows = left_panel.shape[0]
    step = rows // CHUNKS

    def kernel(parts_ref, left_ref, weights_ref, out_ref, scaled, left, sems):
        def copy(n):
            chunk = pl.ds(n * step, step)
            return pltpu.make_async_copy(left_ref.at[chunk, :], left.at[chunk, :], sems.at[n])

        for n in range(CHUNKS):
            copy(n).start()
        lane = lax.broadcasted_iota(jnp.int32, (SET, LANES), 1) // PART
        for g in range(4):
            held = [parts_ref[(4 * g + sub) // 2, sub % 2].astype(F32) for sub in range(4)]
            for m in range(MB):
                whole = held[m]
                for sub in range(4):
                    if sub != m:
                        whole = jnp.where(lane == sub, pltpu.roll(held[sub], (sub - m) % 4 * PART, 1), whole)
                at = (m * 4 + g) * LANES
                for f in range(2):
                    scaled[f * SET : (f + 1) * SET, at : at + LANES] = (
                        whole * weights_ref[f : f + 1, at : at + LANES]
                    ).astype(BF16)
        for n in range(CHUNKS):
            copy(n).wait()
            product = lax.dot_general(
                scaled[...], left[n * step : (n + 1) * step, :], (((1,), (1,)), ((), ())), preferred_element_type=F32
            )
            out_ref[0, :, n * step : (n + 1) * step] = product[:SET]
            out_ref[1, :, n * step : (n + 1) * step] = product[SET:]

    return pl.pallas_call(
        kernel,
        out_shape=jax.ShapeDtypeStruct((2, SET, rows), F32),
        in_specs=[VMEM, pl.BlockSpec(memory_space=pl.ANY), VMEM],
        out_specs=VMEM,
        scratch_shapes=[
            pltpu.VMEM((2 * SET, NPAIR), BF16),
            pltpu.VMEM((rows, NPAIR), BF16),
            pltpu.SemaphoreType.DMA((CHUNKS,)),
        ],
        compiler_params=pltpu.CompilerParams(vmem_limit_bytes=56 << 20),
        name="screened_response",
    )(parts, left_panel, weights)


def shards(
    tiles, tile_blocks, tile_pairs, tile_counts, left_panel, gaps, times, cos_weights, bank, probe_idx
):
    with jax.named_scope("parts"):
        parts = outgoing_parts(tiles, tile_blocks.reshape(SLOTS), tile_pairs, tile_counts)
        parts = lax.all_to_all(parts, ("u", "z"), 0, 0, tiled=True)
    with jax.named_scope("probes"):
        banked = lax.all_gather(bank, "y", axis=0)
        other = lax.ppermute(banked, "k", [(0, 1), (1, 0)])
        probes, weights = picked_probes(
            banked, other, probe_idx.reshape(1, NPROBE), gaps.reshape(1, NPAIR), times, cos_weights
        )
    with jax.named_scope("products"):
        products = owner_products(parts, probes)
        products = lax.all_to_all(products, ("u", "z"), 0, 0, tiled=True)
        product = jnp.sum(products.astype(F32), axis=0).astype(BF16)
    with jax.named_scope("spread"):
        both = lax.all_gather(product, "k", axis=0)
        both = lax.all_to_all(jnp.broadcast_to(both, (8,) + both.shape), ("f", "y"), 0, 0, tiled=True)
    with jax.named_scope("response"):
        turned = screened_response(both, left_panel, weights)
        return jnp.swapaxes(turned, 1, 2)


def solution(mesh):
    fine = Mesh(mesh.devices.reshape(2, 4, 2, 2, 8), ("f", "y", "k", "u", "z"))
    row, col = ("y", "k"), ("u", "z")
    placed = (
        P(col, None, None),
        P(col, None),
        P(col),
        P(col),
        P(row, None),
        P(),
        P(),
        P(),
        P(col, row),
        P(),
    )
    return jax.shard_map(
        shards, mesh=fine, in_specs=placed, out_specs=P("f", row, col), check_vma=False
    )
```

```python
import jax
import jax.numpy as jnp
from jax import lax
from jax.experimental import pallas as pl
from jax.experimental.pallas import tpu as pltpu
from jax.sharding import Mesh, PartitionSpec as P

TILE = 512
MB = 4
CAP = 2
SLOTS = 16
NB = 16
NPAIR = 2048
NPROBE = 512
SET = 32
PART = 32
CODE = 16
LANES = 128
UNIT = PART * TILE // LANES
ROWS = CAP * UNIT + CODE
F32 = jnp.float32
BF16 = jnp.bfloat16
SMEM = pl.BlockSpec(memory_space=pltpu.SMEM)
VMEM = pl.BlockSpec(memory_space=pltpu.VMEM)
HBM = pl.BlockSpec(memory_space=pltpu.HBM)


def place():
    return lax.axis_index("f") * 8 + lax.axis_index("y") * 2 + lax.axis_index("k")


def outgoing_parts(tiles, blocks, pairs, counts):
    def kernel(blocks_ref, pairs_ref, counts_ref, tiles_ref, out_ref, held, parts, source, sems):
        me = place()
        lanes = pl.ds(pl.multiple_of(me // 4 * LANES, LANES), LANES)

        def copy(s):
            return pltpu.make_async_copy(tiles_ref.at[s, :, lanes], held.at[s], sems.at[s])

        for s in range(SLOTS):
            copy(s).start()
        live = counts_ref[0]
        for d in range(NB * CAP):
            source[d] = -1
        for s in range(SLOTS):
            at = blocks_ref[s] * CAP
            at = jnp.where(source[at] >= 0, at + 1, at)
            source[at] = jnp.where(s < live, s, source[at])

        wanted = lax.broadcasted_iota(jnp.int32, (PART, LANES), 0) + me % 4 * PART
        pick = jnp.where(wanted == lax.broadcasted_iota(jnp.int32, (PART, LANES), 1), 1.0, 0.0).astype(BF16)
        for s in range(SLOTS):
            copy(s).wait()
        for s in range(SLOTS):
            part = lax.dot_general(pick, held[s], (((1,), (1,)), ((), ())), preferred_element_type=F32)
            for n in range(TILE // LANES):
                parts[s, n * PART : (n + 1) * PART, :] = part[:, n * LANES : (n + 1) * LANES].astype(BF16)

        second = lax.broadcasted_iota(jnp.int32, (CODE, LANES), 0) >= CODE // CAP
        for d in range(NB):
            codes = []
            for j in range(CAP):
                s = source[d * CAP + j]
                there = jnp.maximum(s, 0)
                full = jnp.where(s >= 0, 1.0, 0.0).astype(BF16)
                out_ref[d, j * UNIT : (j + 1) * UNIT, :] = parts[there] * full
                codes.append(pairs_ref[there].astype(F32))
            out_ref[d, CAP * UNIT :, :] = jnp.where(second, codes[1], codes[0]).astype(BF16)

    return pl.pallas_call(
        kernel,
        out_shape=jax.ShapeDtypeStruct((NB, ROWS, LANES), BF16),
        in_specs=[SMEM, SMEM, SMEM, HBM],
        out_specs=VMEM,
        scratch_shapes=[
            pltpu.VMEM((SLOTS, TILE, LANES), BF16),
            pltpu.VMEM((SLOTS, UNIT, LANES), BF16),
            pltpu.SMEM((NB * CAP,), jnp.int32),
            pltpu.SemaphoreType.DMA((SLOTS,)),
        ],
        compiler_params=pltpu.CompilerParams(vmem_limit_bytes=8 << 20),
        name="outgoing_parts",
    )(blocks, pairs, counts, tiles)


def picked_probes(own, other, probe_idx, gaps, times, cos_weights):
    def kernel(times_ref, cos_ref, own_ref, other_ref, idx_ref, gaps_ref, out_ref, weights_ref):
        core = lax.axis_index("k")
        total = jnp.zeros((TILE, NPROBE), F32)
        for bank_ref, at in ((own_ref, core), (other_ref, 1 - core)):
            for y in range(4):
                here = lax.broadcasted_iota(jnp.int32, (LANES, NPROBE), 0) + (y * 2 + at) * LANES
                pick = jnp.where(here == idx_ref[...], 1.0, 0.0).astype(BF16)
                total += jnp.dot(bank_ref[y], pick, preferred_element_type=F32)
        out_ref[...] = total.astype(BF16)
        first = lax.axis_index("f") * 2
        decays = [jnp.exp(-gaps_ref[...] * times_ref[k]) for k in range(4)]
        for f in range(2):
            weight = decays[0] * cos_ref[first + f, 0]
            for k in range(1, 4):
                weight += decays[k] * cos_ref[first + f, k]
            weights_ref[f : f + 1, :] = weight

    return pl.pallas_call(
        kernel,
        out_shape=(jax.ShapeDtypeStruct((TILE, NPROBE), BF16), jax.ShapeDtypeStruct((2, NPAIR), F32)),
        in_specs=[SMEM, SMEM, VMEM, VMEM, VMEM, VMEM],
        out_specs=(VMEM, VMEM),
        compiler_params=pltpu.CompilerParams(vmem_limit_bytes=24 << 20),
        name="picked_probes",
    )(times, cos_weights, own, other, probe_idx, gaps)


def owner_products(parts, probes, left_panel):
    half = left_panel.shape[0] // 2

    def kernel(parts_ref, probes_ref, left_ref, out_ref, left_out_ref, held, product, sems):
        first = pltpu.make_async_copy(probes_ref, held, sems.at[0])
        first.start()
        fetch = pltpu.make_async_copy(left_ref.at[pl.ds(0, half), :], left_out_ref, sems.at[1])
        units = parts_ref[:, : CAP * UNIT, :].reshape(NB * CAP, TILE // LANES, PART, LANES)
        rows = jnp.concatenate([units[:, n] for n in range(TILE // LANES)], axis=-1).reshape(NB * CAP * PART, TILE)
        first.wait()
        fetch.start()
        product[...] = jnp.dot(rows, held[...], preferred_element_type=F32)
        codes = [
            parts_ref[c, CAP * UNIT :, :].astype(F32)[j * (CODE // CAP) : j * (CODE // CAP) + 1, :1]
            for c in range(NB)
            for j in range(CAP)
        ]
        for m in range(MB):
            total = jnp.zeros((PART, NPROBE), F32)
            for n, code in enumerate(codes):
                total += jnp.where(code == m, product[n * PART : (n + 1) * PART, :], 0.0)
            turned = total.T.astype(BF16)
            for c in range(NB):
                out_ref[c, :, m * PART : (m + 1) * PART] = turned[c * SET : (c + 1) * SET, :]
        fetch.wait()

    return pl.pallas_call(
        kernel,
        out_shape=(
            jax.ShapeDtypeStruct((NB, SET, MB * PART), BF16),
            jax.ShapeDtypeStruct((half, NPAIR), BF16),
        ),
        in_specs=[VMEM, HBM, HBM],
        out_specs=(VMEM, VMEM),
        scratch_shapes=[
            pltpu.VMEM((TILE, NPROBE), BF16),
            pltpu.VMEM((NB * CAP * PART, NPROBE), F32),
            pltpu.SemaphoreType.DMA((2,)),
        ],
        compiler_params=pltpu.CompilerParams(vmem_limit_bytes=16 << 20),
        name="owner_products",
    )(parts, probes, left_panel)


def screened_response(parts, first_half, left_panel, weights):
    half = first_half.shape[0]

    def kernel(parts_ref, first_ref, left_ref, weights_ref, out_ref, scaled, second, sem):
        fetch = pltpu.make_async_copy(left_ref.at[pl.ds(half, half), :], second, sem)
        fetch.start()
        lane = lax.broadcasted_iota(jnp.int32, (SET, LANES), 1) // PART
        for g in range(4):
            held = [parts_ref[(4 * g + sub) // 2, sub % 2].astype(F32) for sub in range(4)]
            for m in range(MB):
                whole = held[m]
                for sub in range(4):
                    if sub != m:
                        whole = jnp.where(lane == sub, pltpu.roll(held[sub], (sub - m) % 4 * PART, 1), whole)
                at = (m * 4 + g) * LANES
                for f in range(2):
                    scaled[f * SET : (f + 1) * SET, at : at + LANES] = (
                        whole * weights_ref[f : f + 1, at : at + LANES]
                    ).astype(BF16)
        for n, left in enumerate((first_ref, second)):
            if n == 1:
                fetch.wait()
            product = lax.dot_general(
                scaled[...], left[...], (((1,), (1,)), ((), ())), preferred_element_type=F32
            )
            out_ref[0, :, n * half : (n + 1) * half] = product[:SET]
            out_ref[1, :, n * half : (n + 1) * half] = product[SET:]

    return pl.pallas_call(
        kernel,
        out_shape=jax.ShapeDtypeStruct((2, SET, 2 * half), F32),
        in_specs=[VMEM, VMEM, HBM, VMEM],
        out_specs=VMEM,
        scratch_shapes=[
            pltpu.VMEM((2 * SET, NPAIR), BF16),
            pltpu.VMEM((half, NPAIR), BF16),
            pltpu.SemaphoreType.DMA,
        ],
        compiler_params=pltpu.CompilerParams(vmem_limit_bytes=12 << 20),
        name="screened_response",
    )(parts, first_half, left_panel, weights)


def shards(
    tiles, tile_blocks, tile_pairs, tile_counts, left_panel, gaps, times, cos_weights, bank, probe_idx
):
    stay = lambda array: pltpu.with_memory_space_constraint(array, pltpu.HBM)
    tiles, tile_blocks, tile_pairs, left_panel = map(stay, (tiles, tile_blocks.reshape(SLOTS), tile_pairs, left_panel))
    with jax.named_scope("parts"):
        parts = outgoing_parts(tiles, tile_blocks, tile_pairs, tile_counts)
        parts = lax.all_to_all(parts, ("u", "z"), 0, 0, tiled=True)
    with jax.named_scope("probes"):
        banked = lax.all_gather(bank, "y", axis=0)
        other = lax.ppermute(banked, "k", [(0, 1), (1, 0)])
        probes, weights = picked_probes(
            banked, other, probe_idx.reshape(1, NPROBE), gaps.reshape(1, NPAIR), times, cos_weights
        )
    with jax.named_scope("products"):
        products, first_half = owner_products(parts, stay(probes), left_panel)
        products = lax.all_to_all(products, ("u", "z"), 0, 0, tiled=True)
        product = jnp.sum(products.astype(F32), axis=0).astype(BF16)
    with jax.named_scope("spread"):
        both = lax.all_gather(product, "k", axis=0)
        both = lax.all_to_all(jnp.broadcast_to(both, (8,) + both.shape), ("f", "y"), 0, 0, tiled=True)
    with jax.named_scope("response"):
        turned = screened_response(both, first_half, left_panel, weights)
        return jnp.swapaxes(turned, 1, 2)


def solution(mesh):
    fine = Mesh(mesh.devices.reshape(2, 4, 2, 2, 8), ("f", "y", "k", "u", "z"))
    row, col = ("y", "k"), ("u", "z")
    placed = (
        P(col, None, None),
        P(col, None),
        P(col),
        P(col),
        P(row, None),
        P(),
        P(),
        P(),
        P(col, row),
        P(),
    )
    return jax.shard_map(
        shards, mesh=fine, in_specs=placed, out_specs=P("f", row, col), check_vma=False
    )
```

```python
import jax
import jax.numpy as jnp
from jax import lax
from jax.experimental import pallas as pl
from jax.experimental.pallas import tpu as pltpu
from jax.sharding import Mesh, PartitionSpec as P

TILE = 512
MB = 4
CAP = 2
SLOTS = 16
NB = 16
NPAIR = 2048
NPROBE = 512
SET = 32
PART = 32
CODE = 16
LANES = 128
UNIT = PART * TILE // LANES
ROWS = CAP * UNIT + CODE
F32 = jnp.float32
BF16 = jnp.bfloat16
SMEM = pl.BlockSpec(memory_space=pltpu.SMEM)
VMEM = pl.BlockSpec(memory_space=pltpu.VMEM)
HBM = pl.BlockSpec(memory_space=pltpu.HBM)


def place():
    return lax.axis_index("f") * 8 + lax.axis_index("y") * 2 + lax.axis_index("k")


def outgoing_parts(tiles, blocks, pairs, counts):
    def kernel(blocks_ref, pairs_ref, counts_ref, tiles_ref, out_ref, held, parts, source, sems):
        me = place()
        lanes = pl.ds(pl.multiple_of(me // 4 * LANES, LANES), LANES)

        def copy(s):
            return pltpu.make_async_copy(tiles_ref.at[s, :, lanes], held.at[s], sems.at[s])

        for s in range(SLOTS):
            copy(s).start()
        live = counts_ref[0]
        for d in range(NB * CAP):
            source[d] = -1
        for s in range(SLOTS):
            at = blocks_ref[s] * CAP
            at = jnp.where(source[at] >= 0, at + 1, at)
            source[at] = jnp.where(s < live, s, source[at])

        wanted = lax.broadcasted_iota(jnp.int32, (PART, LANES), 0) + me % 4 * PART
        pick = jnp.where(wanted == lax.broadcasted_iota(jnp.int32, (PART, LANES), 1), 1.0, 0.0).astype(BF16)
        for s in range(SLOTS):
            copy(s).wait()
        for s in range(SLOTS):
            part = lax.dot_general(pick, held[s], (((1,), (1,)), ((), ())), preferred_element_type=F32)
            for n in range(TILE // LANES):
                parts[s, n * PART : (n + 1) * PART, :] = part[:, n * LANES : (n + 1) * LANES].astype(BF16)

        second = lax.broadcasted_iota(jnp.int32, (CODE, LANES), 0) >= CODE // CAP
        for d in range(NB):
            codes = []
            for j in range(CAP):
                s = source[d * CAP + j]
                there = jnp.maximum(s, 0)
                full = jnp.where(s >= 0, 1.0, 0.0).astype(BF16)
                out_ref[d, j * UNIT : (j + 1) * UNIT, :] = parts[there] * full
                codes.append(pairs_ref[there].astype(F32))
            out_ref[d, CAP * UNIT :, :] = jnp.where(second, codes[1], codes[0]).astype(BF16)

    return pl.pallas_call(
        kernel,
        out_shape=jax.ShapeDtypeStruct((NB, ROWS, LANES), BF16),
        in_specs=[SMEM, SMEM, SMEM, HBM],
        out_specs=VMEM,
        scratch_shapes=[
            pltpu.VMEM((SLOTS, TILE, LANES), BF16),
            pltpu.VMEM((SLOTS, UNIT, LANES), BF16),
            pltpu.SMEM((NB * CAP,), jnp.int32),
            pltpu.SemaphoreType.DMA((SLOTS,)),
        ],
        compiler_params=pltpu.CompilerParams(vmem_limit_bytes=8 << 20),
        name="outgoing_parts",
    )(blocks, pairs, counts, tiles)


def picked_probes(own, other, probe_idx, gaps, times, cos_weights, left_panel):
    half = left_panel.shape[0] // 2

    def kernel(
        times_ref, cos_ref, own_ref, other_ref, idx_ref, gaps_ref, left_ref, out_ref, weights_ref, first_ref, sem
    ):
        fetch = pltpu.make_async_copy(left_ref.at[pl.ds(0, half), :], first_ref, sem)
        fetch.start()
        core = lax.axis_index("k")
        total = jnp.zeros((TILE, NPROBE), F32)
        for bank_ref, at in ((own_ref, core), (other_ref, 1 - core)):
            for y in range(4):
                here = lax.broadcasted_iota(jnp.int32, (LANES, NPROBE), 0) + (y * 2 + at) * LANES
                pick = jnp.where(here == idx_ref[...], 1.0, 0.0).astype(BF16)
                total += jnp.dot(bank_ref[y], pick, preferred_element_type=F32)
        out_ref[...] = total.astype(BF16)
        first = lax.axis_index("f") * 2
        decays = [jnp.exp(-gaps_ref[...] * times_ref[k]) for k in range(4)]
        for f in range(2):
            weight = decays[0] * cos_ref[first + f, 0]
            for k in range(1, 4):
                weight += decays[k] * cos_ref[first + f, k]
            weights_ref[f : f + 1, :] = weight
        fetch.wait()

    return pl.pallas_call(
        kernel,
        out_shape=(
            jax.ShapeDtypeStruct((TILE, NPROBE), BF16),
            jax.ShapeDtypeStruct((2, NPAIR), F32),
            jax.ShapeDtypeStruct((half, NPAIR), BF16),
        ),
        in_specs=[SMEM, SMEM, VMEM, VMEM, VMEM, VMEM, HBM],
        out_specs=(VMEM, VMEM, VMEM),
        scratch_shapes=[pltpu.SemaphoreType.DMA],
        compiler_params=pltpu.CompilerParams(vmem_limit_bytes=24 << 20),
        name="picked_probes",
    )(times, cos_weights, own, other, probe_idx, gaps, left_panel)


def owner_products(parts, probes):
    def kernel(parts_ref, probes_ref, out_ref, held, product, sem):
        fetch = pltpu.make_async_copy(probes_ref, held, sem)
        fetch.start()
        units = parts_ref[:, : CAP * UNIT, :].reshape(NB * CAP, TILE // LANES, PART, LANES)
        rows = jnp.concatenate([units[:, n] for n in range(TILE // LANES)], axis=-1).reshape(NB * CAP * PART, TILE)
        fetch.wait()
        product[...] = jnp.dot(rows, held[...], preferred_element_type=F32)
        codes = [
            parts_ref[c, CAP * UNIT :, :].astype(F32)[j * (CODE // CAP) : j * (CODE // CAP) + 1, :1]
            for c in range(NB)
            for j in range(CAP)
        ]
        for m in range(MB):
            total = jnp.zeros((PART, NPROBE), F32)
            for n, code in enumerate(codes):
                total += jnp.where(code == m, product[n * PART : (n + 1) * PART, :], 0.0)
            turned = total.T.astype(BF16)
            for c in range(NB):
                out_ref[c, :, m * PART : (m + 1) * PART] = turned[c * SET : (c + 1) * SET, :]

    return pl.pallas_call(
        kernel,
        out_shape=jax.ShapeDtypeStruct((NB, SET, MB * PART), BF16),
        in_specs=[VMEM, HBM],
        out_specs=VMEM,
        scratch_shapes=[
            pltpu.VMEM((TILE, NPROBE), BF16),
            pltpu.VMEM((NB * CAP * PART, NPROBE), F32),
            pltpu.SemaphoreType.DMA,
        ],
        compiler_params=pltpu.CompilerParams(vmem_limit_bytes=16 << 20),
        name="owner_products",
    )(parts, probes)


def screened_response(parts, first_half, left_panel, weights):
    half = first_half.shape[0]

    def kernel(parts_ref, first_ref, left_ref, weights_ref, out_ref, scaled, second, sem):
        fetch = pltpu.make_async_copy(left_ref.at[pl.ds(half, half), :], second, sem)
        fetch.start()
        lane = lax.broadcasted_iota(jnp.int32, (SET, LANES), 1) // PART
        for g in range(4):
            held = [parts_ref[(4 * g + sub) // 2, sub % 2].astype(F32) for sub in range(4)]
            for m in range(MB):
                whole = held[m]
                for sub in range(4):
                    if sub != m:
                        whole = jnp.where(lane == sub, pltpu.roll(held[sub], (sub - m) % 4 * PART, 1), whole)
                at = (m * 4 + g) * LANES
                for f in range(2):
                    scaled[f * SET : (f + 1) * SET, at : at + LANES] = (
                        whole * weights_ref[f : f + 1, at : at + LANES]
                    ).astype(BF16)
        for n, left in enumerate((first_ref, second)):
            if n == 1:
                fetch.wait()
            product = lax.dot_general(
                scaled[...], left[...], (((1,), (1,)), ((), ())), preferred_element_type=F32
            )
            out_ref[0, :, n * half : (n + 1) * half] = product[:SET]
            out_ref[1, :, n * half : (n + 1) * half] = product[SET:]

    return pl.pallas_call(
        kernel,
        out_shape=jax.ShapeDtypeStruct((2, SET, 2 * half), F32),
        in_specs=[VMEM, VMEM, HBM, VMEM],
        out_specs=VMEM,
        scratch_shapes=[
            pltpu.VMEM((2 * SET, NPAIR), BF16),
            pltpu.VMEM((half, NPAIR), BF16),
            pltpu.SemaphoreType.DMA,
        ],
        compiler_params=pltpu.CompilerParams(vmem_limit_bytes=12 << 20),
        name="screened_response",
    )(parts, first_half, left_panel, weights)


def shards(
    tiles, tile_blocks, tile_pairs, tile_counts, left_panel, gaps, times, cos_weights, bank, probe_idx
):
    stay = lambda array: pltpu.with_memory_space_constraint(array, pltpu.HBM)
    tiles, tile_blocks, tile_pairs, left_panel = map(stay, (tiles, tile_blocks.reshape(SLOTS), tile_pairs, left_panel))
    with jax.named_scope("parts"):
        parts = outgoing_parts(tiles, tile_blocks, tile_pairs, tile_counts)
        parts = lax.all_to_all(parts, ("u", "z"), 0, 0, tiled=True)
    with jax.named_scope("probes"):
        banked = lax.all_gather(bank, "y", axis=0)
        other = lax.ppermute(banked, "k", [(0, 1), (1, 0)])
        probes, weights, first_half = picked_probes(
            banked, other, probe_idx.reshape(1, NPROBE), gaps.reshape(1, NPAIR), times, cos_weights, left_panel
        )
    with jax.named_scope("products"):
        products = owner_products(parts, stay(probes))
        products = lax.all_to_all(products, ("u", "z"), 0, 0, tiled=True)
        product = jnp.sum(products.astype(F32), axis=0).astype(BF16)
    with jax.named_scope("spread"):
        both = lax.all_gather(product, "k", axis=0)
        both = lax.all_to_all(jnp.broadcast_to(both, (8,) + both.shape), ("f", "y"), 0, 0, tiled=True)
    with jax.named_scope("response"):
        turned = screened_response(both, first_half, left_panel, weights)
        return jnp.swapaxes(turned, 1, 2)


def solution(mesh):
    fine = Mesh(mesh.devices.reshape(2, 4, 2, 2, 8), ("f", "y", "k", "u", "z"))
    row, col = ("y", "k"), ("u", "z")
    placed = (
        P(col, None, None),
        P(col, None),
        P(col),
        P(col),
        P(row, None),
        P(),
        P(),
        P(),
        P(col, row),
        P(),
    )
    return jax.shard_map(
        shards, mesh=fine, in_specs=placed, out_specs=P("f", row, col), check_vma=False
    )
```

```python
import jax
import jax.numpy as jnp
from jax import lax
from jax.experimental import pallas as pl
from jax.experimental.pallas import tpu as pltpu
from jax.sharding import Mesh, PartitionSpec as P

TILE = 512
MB = 4
CAP = 2
SLOTS = 16
NB = 16
NPAIR = 2048
NPROBE = 512
SET = 32
PART = 32
CODE = 16
LANES = 128
UNIT = PART * TILE // LANES
ROWS = CAP * UNIT + CODE
F32 = jnp.float32
BF16 = jnp.bfloat16
SMEM = pl.BlockSpec(memory_space=pltpu.SMEM)
VMEM = pl.BlockSpec(memory_space=pltpu.VMEM)
HBM = pl.BlockSpec(memory_space=pltpu.HBM)


def place():
    return lax.axis_index("f") * 8 + lax.axis_index("y") * 2 + lax.axis_index("k")


def outgoing_parts(tiles, blocks, pairs, counts):
    def kernel(blocks_ref, pairs_ref, counts_ref, tiles_ref, out_ref, held, parts, source, placed, sems, out_sems):
        me = place()
        lanes = pl.ds(pl.multiple_of(me // 4 * LANES, LANES), LANES)

        def copy(s):
            return pltpu.make_async_copy(tiles_ref.at[s, :, lanes], held.at[s], sems.at[s])

        def sent(d):
            return pltpu.make_async_copy(placed.at[d], out_ref.at[d], out_sems.at[d])

        for s in range(SLOTS):
            copy(s).start()
        live = counts_ref[0]
        for d in range(NB * CAP):
            source[d] = -1
        for s in range(SLOTS):
            at = blocks_ref[s] * CAP
            at = jnp.where(source[at] >= 0, at + 1, at)
            source[at] = jnp.where(s < live, s, source[at])

        wanted = lax.broadcasted_iota(jnp.int32, (PART, LANES), 0) + me % 4 * PART
        pick = jnp.where(wanted == lax.broadcasted_iota(jnp.int32, (PART, LANES), 1), 1.0, 0.0).astype(BF16)
        for s in range(SLOTS):
            copy(s).wait()
        for s in range(SLOTS):
            part = lax.dot_general(pick, held[s], (((1,), (1,)), ((), ())), preferred_element_type=F32)
            for n in range(TILE // LANES):
                parts[s, n * PART : (n + 1) * PART, :] = part[:, n * LANES : (n + 1) * LANES].astype(BF16)

        second = lax.broadcasted_iota(jnp.int32, (CODE, LANES), 0) >= CODE // CAP
        for d in range(NB):
            codes = []
            for j in range(CAP):
                s = source[d * CAP + j]
                there = jnp.maximum(s, 0)
                full = jnp.where(s >= 0, 1.0, 0.0).astype(BF16)
                placed[d, j * UNIT : (j + 1) * UNIT, :] = parts[there] * full
                codes.append(pairs_ref[there].astype(F32))
            placed[d, CAP * UNIT :, :] = jnp.where(second, codes[1], codes[0]).astype(BF16)
            sent(d).start()
        for d in range(NB):
            sent(d).wait()

    return pl.pallas_call(
        kernel,
        out_shape=jax.ShapeDtypeStruct((NB, ROWS, LANES), BF16),
        in_specs=[SMEM, SMEM, SMEM, HBM],
        out_specs=HBM,
        scratch_shapes=[
            pltpu.VMEM((SLOTS, TILE, LANES), BF16),
            pltpu.VMEM((SLOTS, UNIT, LANES), BF16),
            pltpu.SMEM((NB * CAP,), jnp.int32),
            pltpu.VMEM((NB, ROWS, LANES), BF16),
            pltpu.SemaphoreType.DMA((SLOTS,)),
            pltpu.SemaphoreType.DMA((NB,)),
        ],
        compiler_params=pltpu.CompilerParams(vmem_limit_bytes=8 << 20),
        name="outgoing_parts",
    )(blocks, pairs, counts, tiles)


def picked_probes(own, other, probe_idx, gaps, times, cos_weights, left_panel):
    cut = left_panel.shape[0] // 2

    def kernel(
        times_ref, cos_ref, own_ref, other_ref, idx_ref, gaps_ref, left_ref, out_ref, weights_ref, first_ref, sem
    ):
        fetch = pltpu.make_async_copy(left_ref.at[pl.ds(0, cut), :], first_ref, sem)
        fetch.start()
        core = lax.axis_index("k")
        total = jnp.zeros((TILE, NPROBE), F32)
        for bank_ref, at in ((own_ref, core), (other_ref, 1 - core)):
            for y in range(4):
                here = lax.broadcasted_iota(jnp.int32, (LANES, NPROBE), 0) + (y * 2 + at) * LANES
                pick = jnp.where(here == idx_ref[...], 1.0, 0.0).astype(BF16)
                total += jnp.dot(bank_ref[y], pick, preferred_element_type=F32)
        out_ref[...] = total.astype(BF16)
        first = lax.axis_index("f") * 2
        decays = [jnp.exp(-gaps_ref[...] * times_ref[k]) for k in range(4)]
        for f in range(2):
            weight = decays[0] * cos_ref[first + f, 0]
            for k in range(1, 4):
                weight += decays[k] * cos_ref[first + f, k]
            weights_ref[f : f + 1, :] = weight
        fetch.wait()

    return pl.pallas_call(
        kernel,
        out_shape=(
            jax.ShapeDtypeStruct((TILE, NPROBE), BF16),
            jax.ShapeDtypeStruct((2, NPAIR), F32),
            jax.ShapeDtypeStruct((cut, NPAIR), BF16),
        ),
        in_specs=[SMEM, SMEM, VMEM, VMEM, VMEM, VMEM, HBM],
        out_specs=(VMEM, VMEM, VMEM),
        scratch_shapes=[pltpu.SemaphoreType.DMA],
        compiler_params=pltpu.CompilerParams(vmem_limit_bytes=24 << 20),
        name="picked_probes",
    )(times, cos_weights, own, other, probe_idx, gaps, left_panel)


def owner_products(parts, probes):
    def kernel(parts_ref, probes_ref, out_ref, held, product, sem):
        fetch = pltpu.make_async_copy(probes_ref, held, sem)
        fetch.start()
        units = parts_ref[:, : CAP * UNIT, :].reshape(NB * CAP, TILE // LANES, PART, LANES)
        rows = jnp.concatenate([units[:, n] for n in range(TILE // LANES)], axis=-1).reshape(NB * CAP * PART, TILE)
        fetch.wait()
        product[...] = jnp.dot(rows, held[...], preferred_element_type=F32)
        codes = [
            parts_ref[c, CAP * UNIT :, :].astype(F32)[j * (CODE // CAP) : j * (CODE // CAP) + 1, :1]
            for c in range(NB)
            for j in range(CAP)
        ]
        for m in range(MB):
            total = jnp.zeros((PART, NPROBE), F32)
            for n, code in enumerate(codes):
                total += jnp.where(code == m, product[n * PART : (n + 1) * PART, :], 0.0)
            turned = total.T.astype(BF16)
            for c in range(NB):
                out_ref[c, :, m * PART : (m + 1) * PART] = turned[c * SET : (c + 1) * SET, :]

    return pl.pallas_call(
        kernel,
        out_shape=jax.ShapeDtypeStruct((NB, SET, MB * PART), BF16),
        in_specs=[VMEM, HBM],
        out_specs=VMEM,
        scratch_shapes=[
            pltpu.VMEM((TILE, NPROBE), BF16),
            pltpu.VMEM((NB * CAP * PART, NPROBE), F32),
            pltpu.SemaphoreType.DMA,
        ],
        compiler_params=pltpu.CompilerParams(vmem_limit_bytes=16 << 20),
        name="owner_products",
    )(parts, probes)


def screened_response(parts, first, left_panel, weights):
    cut, rows = first.shape[0], left_panel.shape[0]

    def kernel(parts_ref, first_ref, left_ref, weights_ref, out_ref, scaled, second, sem):
        fetch = pltpu.make_async_copy(left_ref.at[pl.ds(cut, rows - cut), :], second, sem)
        fetch.start()
        core = lax.axis_index("k")
        lane = lax.broadcasted_iota(jnp.int32, (SET, LANES), 1) // PART
        for g in range(4):
            held = [parts_ref[2 * g + sub // 2, jnp.abs(core - sub % 2)].astype(F32) for sub in range(4)]
            for m in range(MB):
                whole = held[m]
                for sub in range(4):
                    if sub != m:
                        whole = jnp.where(lane == sub, pltpu.roll(held[sub], (sub - m) % 4 * PART, 1), whole)
                at = (m * 4 + g) * LANES
                for f in range(2):
                    scaled[f * SET : (f + 1) * SET, at : at + LANES] = (
                        whole * weights_ref[f : f + 1, at : at + LANES]
                    ).astype(BF16)
        for left, start, stop in ((first_ref, 0, cut), (second, cut, rows)):
            if start == cut:
                fetch.wait()
            product = lax.dot_general(
                scaled[...], left[...], (((1,), (1,)), ((), ())), preferred_element_type=F32
            )
            out_ref[0, :, start:stop] = product[:SET]
            out_ref[1, :, start:stop] = product[SET:]

    return pl.pallas_call(
        kernel,
        out_shape=jax.ShapeDtypeStruct((2, SET, rows), F32),
        in_specs=[VMEM, VMEM, HBM, VMEM],
        out_specs=VMEM,
        scratch_shapes=[
            pltpu.VMEM((2 * SET, NPAIR), BF16),
            pltpu.VMEM((rows - cut, NPAIR), BF16),
            pltpu.SemaphoreType.DMA,
        ],
        compiler_params=pltpu.CompilerParams(vmem_limit_bytes=12 << 20),
        name="screened_response",
    )(parts, first, left_panel, weights)


def shards(
    tiles, tile_blocks, tile_pairs, tile_counts, left_panel, gaps, times, cos_weights, bank, probe_idx
):
    stay = lambda array: pltpu.with_memory_space_constraint(array, pltpu.HBM)
    tiles, tile_blocks, tile_pairs, left_panel = map(stay, (tiles, tile_blocks.reshape(SLOTS), tile_pairs, left_panel))
    with jax.named_scope("parts"):
        parts = outgoing_parts(tiles, tile_blocks, tile_pairs, tile_counts)
        parts = lax.all_to_all(parts, ("u", "z"), 0, 0, tiled=True)
    with jax.named_scope("probes"):
        banked = lax.all_gather(bank, "y", axis=0)
        other = lax.ppermute(banked, "k", [(0, 1), (1, 0)])
        probes, weights, first = picked_probes(
            banked, other, probe_idx.reshape(1, NPROBE), gaps.reshape(1, NPAIR), times, cos_weights, left_panel
        )
    with jax.named_scope("products"):
        products = owner_products(parts, stay(probes))
        products = lax.all_to_all(products, ("u", "z"), 0, 0, tiled=True)
        product = jnp.sum(products.astype(F32), axis=0).astype(BF16)
    with jax.named_scope("spread"):
        both = jnp.stack([product, lax.ppermute(product, "k", [(0, 1), (1, 0)])])
        both = lax.all_to_all(jnp.broadcast_to(both, (8,) + both.shape), ("f", "y"), 0, 0, tiled=True)
    with jax.named_scope("response"):
        turned = screened_response(both, first, left_panel, weights)
        return jnp.swapaxes(turned, 1, 2)


def solution(mesh):
    fine = Mesh(mesh.devices.reshape(2, 4, 2, 2, 8), ("f", "y", "k", "u", "z"))
    row, col = ("y", "k"), ("u", "z")
    placed = (
        P(col, None, None),
        P(col, None),
        P(col),
        P(col),
        P(row, None),
        P(),
        P(),
        P(),
        P(col, row),
        P(),
    )
    return jax.shard_map(
        shards, mesh=fine, in_specs=placed, out_specs=P("f", row, col), check_vma=False
    )
```

```python
import jax
import jax.numpy as jnp
from jax import lax
from jax.experimental import pallas as pl
from jax.experimental.pallas import tpu as pltpu
from jax.sharding import Mesh, PartitionSpec as P

TILE = 512
MB = 4
CAP = 2
SLOTS = 16
NB = 16
NPAIR = 2048
NPROBE = 512
SET = 32
PART = 64
GROUP = 8
CODE = 16
LANES = 128
UNIT = PART * TILE // LANES
ROWS = CAP * UNIT + CODE
F32 = jnp.float32
BF16 = jnp.bfloat16
SMEM = pl.BlockSpec(memory_space=pltpu.SMEM)
VMEM = pl.BlockSpec(memory_space=pltpu.VMEM)
HBM = pl.BlockSpec(memory_space=pltpu.HBM)


def runs():
    return [[k * 16 + u * 8 + (2 * k + 4 * h + p) % 8 for u in range(2) for p in range(4)] for k in range(2) for h in range(2)]


def outgoing_parts(tiles, blocks, pairs, counts):
    def kernel(blocks_ref, pairs_ref, counts_ref, tiles_ref, out_ref, held, parts, source, sems):
        core = lax.axis_index("k")
        lanes = pl.ds(pl.multiple_of(lax.axis_index("y") * LANES, LANES), LANES)

        def copy(s):
            return pltpu.make_async_copy(tiles_ref.at[s, :, lanes], held.at[s], sems.at[s])

        for s in range(SLOTS):
            copy(s).start()
        live = counts_ref[0]
        far = lax.axis_index("f")
        run = (lax.axis_index("z") + 8 - 2 * core) % 8 // 4
        for d in range(GROUP * CAP):
            source[d] = -1
        for s in range(SLOTS):
            block = blocks_ref[s]
            along = (block % 8 + 8 - 2 * core) % 8
            mine = jnp.where(along // 4 == run, 0, 1) == far
            at = (block // 8 * 4 + along % 4) * CAP
            at = jnp.where(source[at] >= 0, at + 1, at)
            source[at] = jnp.where(jnp.logical_and(s < live, mine), s, source[at])

        wanted = lax.broadcasted_iota(jnp.int32, (PART, LANES), 0) + core * PART
        pick = jnp.where(wanted == lax.broadcasted_iota(jnp.int32, (PART, LANES), 1), 1.0, 0.0).astype(BF16)
        for s in range(SLOTS):
            copy(s).wait()
        for s in range(SLOTS):
            part = lax.dot_general(pick, held[s], (((1,), (1,)), ((), ())), preferred_element_type=F32)
            for n in range(TILE // LANES):
                parts[s, n * PART : (n + 1) * PART, :] = part[:, n * LANES : (n + 1) * LANES].astype(BF16)

        second = lax.broadcasted_iota(jnp.int32, (CODE, LANES), 0) >= CODE // CAP
        for d in range(GROUP):
            codes = []
            for j in range(CAP):
                s = source[d * CAP + j]
                there = jnp.maximum(s, 0)
                full = jnp.where(s >= 0, 1.0, 0.0).astype(BF16)
                out_ref[d, j * UNIT : (j + 1) * UNIT, :] = parts[there] * full
                codes.append(pairs_ref[there].astype(F32))
            out_ref[d, CAP * UNIT :, :] = jnp.where(second, codes[1], codes[0]).astype(BF16)

    return pl.pallas_call(
        kernel,
        out_shape=jax.ShapeDtypeStruct((GROUP, ROWS, LANES), BF16),
        in_specs=[SMEM, SMEM, SMEM, HBM],
        out_specs=VMEM,
        scratch_shapes=[
            pltpu.VMEM((SLOTS, TILE, LANES), BF16),
            pltpu.VMEM((SLOTS, UNIT, LANES), BF16),
            pltpu.SMEM((GROUP * CAP,), jnp.int32),
            pltpu.SemaphoreType.DMA((SLOTS,)),
        ],
        compiler_params=pltpu.CompilerParams(vmem_limit_bytes=8 << 20),
        name="outgoing_parts",
    )(blocks, pairs, counts, tiles)


def picked_probes(own, other, probe_idx, gaps, times, cos_weights, left_panel):
    half = left_panel.shape[0] // 2

    def kernel(times_ref, cos_ref, *refs):
        bank_refs, (idx_ref, gaps_ref, left_ref, out_ref, weights_ref, first_ref, sem) = refs[:8], refs[8:]
        fetch = pltpu.make_async_copy(left_ref.at[pl.ds(0, half), :], first_ref, sem)
        fetch.start()
        core, y = lax.axis_index("k"), lax.axis_index("y")
        total = jnp.zeros((TILE, NPROBE), F32)
        for n, bank_ref in enumerate(bank_refs):
            row = (y + 4 - n % 4) % 4 * 2 + (core if n < 4 else 1 - core)
            here = lax.broadcasted_iota(jnp.int32, (LANES, NPROBE), 0) + row * LANES
            pick = jnp.where(here == idx_ref[...], 1.0, 0.0).astype(BF16)
            total += jnp.dot(bank_ref[...], pick, preferred_element_type=F32)
        out_ref[...] = total.astype(BF16)
        first = lax.axis_index("f") * 2
        decays = [jnp.exp(-gaps_ref[...] * times_ref[k]) for k in range(4)]
        for f in range(2):
            weight = decays[0] * cos_ref[first + f, 0]
            for k in range(1, 4):
                weight += decays[k] * cos_ref[first + f, k]
            weights_ref[f : f + 1, :] = weight
        fetch.wait()

    return pl.pallas_call(
        kernel,
        out_shape=(
            jax.ShapeDtypeStruct((TILE, NPROBE), BF16),
            jax.ShapeDtypeStruct((2, NPAIR), F32),
            jax.ShapeDtypeStruct((half, NPAIR), BF16),
        ),
        in_specs=[SMEM, SMEM] + [VMEM] * 10 + [HBM],
        out_specs=(VMEM, VMEM, VMEM),
        scratch_shapes=[pltpu.SemaphoreType.DMA],
        compiler_params=pltpu.CompilerParams(vmem_limit_bytes=24 << 20),
        name="picked_probes",
    )(times, cos_weights, *own, *other, probe_idx, gaps, left_panel)


def owner_products(parts, probes):
    def kernel(parts_ref, probes_ref, out_ref, held, product, sem):
        fetch = pltpu.make_async_copy(probes_ref, held, sem)
        fetch.start()
        units = parts_ref[:, : CAP * UNIT, :].reshape(GROUP * CAP, TILE // LANES, PART, LANES)
        rows = jnp.concatenate([units[:, n] for n in range(TILE // LANES)], axis=-1).reshape(GROUP * CAP * PART, TILE)
        fetch.wait()
        product[...] = jnp.dot(rows, held[...], preferred_element_type=F32)
        codes = [
            parts_ref[c, CAP * UNIT :, :].astype(F32)[j * (CODE // CAP) : j * (CODE // CAP) + 1, :1]
            for c in range(GROUP)
            for j in range(CAP)
        ]
        for m in range(MB):
            total = jnp.zeros((PART, NPROBE), F32)
            for n, code in enumerate(codes):
                total += jnp.where(code == m, product[n * PART : (n + 1) * PART, :], 0.0)
            turned = total.T.astype(BF16)
            for c in range(NB):
                out_ref[c, :, m * PART : (m + 1) * PART] = turned[c * SET : (c + 1) * SET, :]

    return pl.pallas_call(
        kernel,
        out_shape=jax.ShapeDtypeStruct((NB, SET, MB * PART), BF16),
        in_specs=[VMEM, HBM],
        out_specs=VMEM,
        scratch_shapes=[
            pltpu.VMEM((TILE, NPROBE), BF16),
            pltpu.VMEM((GROUP * CAP * PART, NPROBE), F32),
            pltpu.SemaphoreType.DMA,
        ],
        compiler_params=pltpu.CompilerParams(vmem_limit_bytes=16 << 20),
        name="owner_products",
    )(parts, probes)


def screened_response(parts, first_half, left_panel, weights):
    half = first_half.shape[0]

    def kernel(parts_ref, first_ref, left_ref, weights_ref, out_ref, scaled, second, sem):
        fetch = pltpu.make_async_copy(left_ref.at[pl.ds(half, half), :], second, sem)
        fetch.start()
        core = lax.axis_index("k")
        low = lax.broadcasted_iota(jnp.int32, (SET, LANES), 1) < PART
        for y in range(4):
            held = [
                parts_ref[y, jnp.abs(core - k)].astype(F32) + parts_ref[4 + y, jnp.abs(core - k)].astype(F32)
                for k in range(2)
            ]
            for m in range(MB):
                start = m // 2 * LANES
                both = [held[k][:, start : start + LANES] for k in range(2)]
                turned = 1 - m % 2
                both[turned] = pltpu.roll(both[turned], PART, 1)
                whole = jnp.where(low, both[0], both[1])
                at = (m * 4 + y) * LANES
                for f in range(2):
                    scaled[f * SET : (f + 1) * SET, at : at + LANES] = (
                        whole * weights_ref[f : f + 1, at : at + LANES]
                    ).astype(BF16)
        for n, left in enumerate((first_ref, second)):
            if n == 1:
                fetch.wait()
            product = lax.dot_general(
                scaled[...], left[...], (((1,), (1,)), ((), ())), preferred_element_type=F32
            )
            out_ref[0, :, n * half : (n + 1) * half] = product[:SET]
            out_ref[1, :, n * half : (n + 1) * half] = product[SET:]

    return pl.pallas_call(
        kernel,
        out_shape=jax.ShapeDtypeStruct((2, SET, 2 * half), F32),
        in_specs=[VMEM, VMEM, HBM, VMEM],
        out_specs=VMEM,
        scratch_shapes=[
            pltpu.VMEM((2 * SET, NPAIR), BF16),
            pltpu.VMEM((half, NPAIR), BF16),
            pltpu.SemaphoreType.DMA,
        ],
        compiler_params=pltpu.CompilerParams(vmem_limit_bytes=12 << 20),
        name="screened_response",
    )(parts, first_half, left_panel, weights)


def shards(
    tiles, tile_blocks, tile_pairs, tile_counts, left_panel, gaps, times, cos_weights, bank, probe_idx
):
    stay = lambda array: pltpu.with_memory_space_constraint(array, pltpu.HBM)
    tiles, tile_blocks, tile_pairs, left_panel = map(stay, (tiles, tile_blocks.reshape(SLOTS), tile_pairs, left_panel))
    swap = [(0, 1), (1, 0)]
    with jax.named_scope("parts"):
        parts = outgoing_parts(tiles, tile_blocks, tile_pairs, tile_counts)
        parts, bank = lax.optimization_barrier((parts, bank))
        parts = lax.all_to_all(parts, ("k", "u", "z"), 0, 0, tiled=True, axis_index_groups=runs())
    with jax.named_scope("probes"):
        owned = [(z, z) for z in range(8)] + [(8 + z, 8 + (z ^ 4)) for z in range(8)]
        bank = lax.ppermute(bank, ("f", "z"), owned)
        own = [bank] + [lax.ppermute(bank, "y", [(y, (y + n) % 4) for y in range(4)]) for n in (1, 2, 3)]
        other = [lax.ppermute(columns, "k", swap) for columns in own]
        probes, weights, first_half = picked_probes(
            own, other, probe_idx.reshape(1, NPROBE), gaps.reshape(1, NPAIR), times, cos_weights, left_panel
        )
    with jax.named_scope("products"):
        products = owner_products(parts, stay(probes))
        products = lax.all_to_all(products, ("u", "z"), 0, 0, tiled=True)
        product = jnp.sum(products.astype(F32), axis=0).astype(BF16)
    with jax.named_scope("spread"):
        both = jnp.stack([product, lax.ppermute(product, "k", swap)])
        both = lax.all_to_all(jnp.broadcast_to(both, (8,) + both.shape), ("f", "y"), 0, 0, tiled=True)
    with jax.named_scope("response"):
        turned = screened_response(both, first_half, left_panel, weights)
        return jnp.swapaxes(turned, 1, 2)


def solution(mesh):
    fine = Mesh(mesh.devices.reshape(2, 4, 2, 2, 8), ("f", "y", "k", "u", "z"))
    row, col = ("y", "k"), ("u", "z")
    placed = (
        P(col, None, None),
        P(col, None),
        P(col),
        P(col),
        P(row, None),
        P(),
        P(),
        P(),
        P(col, row),
        P(),
    )
    return jax.shard_map(
        shards, mesh=fine, in_specs=placed, out_specs=P("f", row, col), check_vma=False
    )
```

```python
import jax
import jax.numpy as jnp
from jax import lax
from jax.experimental import pallas as pl
from jax.experimental.pallas import tpu as pltpu
from jax.sharding import Mesh, PartitionSpec as P

TILE = 512
MB = 4
CAP = 2
SLOTS = 16
NB = 16
NPAIR = 2048
NPROBE = 512
SET = 32
PART = 64
GROUP = 8
CODE = 16
LANES = 128
UNIT = PART * TILE // LANES
ROWS = CAP * UNIT + CODE
F32 = jnp.float32
BF16 = jnp.bfloat16
SMEM = pl.BlockSpec(memory_space=pltpu.SMEM)
VMEM = pl.BlockSpec(memory_space=pltpu.VMEM)
HBM = pl.BlockSpec(memory_space=pltpu.HBM)


def runs():
    return [[k * 16 + u * 8 + (2 * k + 4 * h + p) % 8 for u in range(2) for p in range(4)] for k in range(2) for h in range(2)]


def outgoing_parts(tiles, blocks, pairs, counts):
    def kernel(blocks_ref, pairs_ref, counts_ref, tiles_ref, out_ref, held, parts, source, sems):
        core = lax.axis_index("k")
        lanes = pl.ds(pl.multiple_of(lax.axis_index("y") * LANES, LANES), LANES)

        def copy(s):
            return pltpu.make_async_copy(tiles_ref.at[s, :, lanes], held.at[s], sems.at[s])

        for s in range(SLOTS):
            copy(s).start()
        live = counts_ref[0]
        far = lax.axis_index("f")
        run = (lax.axis_index("z") + 8 - 2 * core) % 8 // 4
        for d in range(GROUP * CAP):
            source[d] = -1
        for s in range(SLOTS):
            block = blocks_ref[s]
            along = (block % 8 + 8 - 2 * core) % 8
            mine = jnp.where(along // 4 == run, 0, 1) == far
            at = (block // 8 * 4 + along % 4) * CAP
            at = jnp.where(source[at] >= 0, at + 1, at)
            source[at] = jnp.where(jnp.logical_and(s < live, mine), s, source[at])

        wanted = lax.broadcasted_iota(jnp.int32, (PART, LANES), 0) + core * PART
        pick = jnp.where(wanted == lax.broadcasted_iota(jnp.int32, (PART, LANES), 1), 1.0, 0.0).astype(BF16)
        for s in range(SLOTS):
            copy(s).wait()
        for s in range(SLOTS):
            part = lax.dot_general(pick, held[s], (((1,), (1,)), ((), ())), preferred_element_type=F32)
            for n in range(TILE // LANES):
                parts[s, n * PART : (n + 1) * PART, :] = part[:, n * LANES : (n + 1) * LANES].astype(BF16)

        second = lax.broadcasted_iota(jnp.int32, (CODE, LANES), 0) >= CODE // CAP
        for d in range(GROUP):
            codes = []
            for j in range(CAP):
                s = source[d * CAP + j]
                there = jnp.maximum(s, 0)
                full = jnp.where(s >= 0, 1.0, 0.0).astype(BF16)
                out_ref[d, j * UNIT : (j + 1) * UNIT, :] = parts[there] * full
                codes.append(pairs_ref[there].astype(F32))
            out_ref[d, CAP * UNIT :, :] = jnp.where(second, codes[1], codes[0]).astype(BF16)

    return pl.pallas_call(
        kernel,
        out_shape=jax.ShapeDtypeStruct((GROUP, ROWS, LANES), BF16),
        in_specs=[SMEM, SMEM, SMEM, HBM],
        out_specs=VMEM,
        scratch_shapes=[
            pltpu.VMEM((SLOTS, TILE, LANES), BF16),
            pltpu.VMEM((SLOTS, UNIT, LANES), BF16),
            pltpu.SMEM((GROUP * CAP,), jnp.int32),
            pltpu.SemaphoreType.DMA((SLOTS,)),
        ],
        compiler_params=pltpu.CompilerParams(vmem_limit_bytes=8 << 20),
        name="outgoing_parts",
    )(blocks, pairs, counts, tiles)


def picked_probes(own, other, probe_idx, gaps, times, cos_weights, left_panel):
    half = left_panel.shape[0] // 2

    def kernel(times_ref, cos_ref, *refs):
        bank_refs, (idx_ref, gaps_ref, left_ref, out_ref, weights_ref, first_ref, sem) = refs[:8], refs[8:]
        fetch = pltpu.make_async_copy(left_ref.at[pl.ds(0, half), :], first_ref, sem)
        fetch.start()
        core, y = lax.axis_index("k"), lax.axis_index("y")
        total = jnp.zeros((TILE, NPROBE), F32)
        for n, bank_ref in enumerate(bank_refs):
            row = (y + 4 - n % 4) % 4 * 2 + (core if n < 4 else 1 - core)
            here = lax.broadcasted_iota(jnp.int32, (LANES, NPROBE), 0) + row * LANES
            pick = jnp.where(here == idx_ref[...], 1.0, 0.0).astype(BF16)
            total += jnp.dot(bank_ref[...], pick, preferred_element_type=F32)
        out_ref[...] = total.astype(BF16)
        first = lax.axis_index("f") * 2
        decays = [jnp.exp(-gaps_ref[...] * times_ref[k]) for k in range(4)]
        for f in range(2):
            weight = decays[0] * cos_ref[first + f, 0]
            for k in range(1, 4):
                weight += decays[k] * cos_ref[first + f, k]
            weights_ref[f : f + 1, :] = weight
        fetch.wait()

    return pl.pallas_call(
        kernel,
        out_shape=(
            jax.ShapeDtypeStruct((TILE, NPROBE), BF16),
            jax.ShapeDtypeStruct((2, NPAIR), F32),
            jax.ShapeDtypeStruct((half, NPAIR), BF16),
        ),
        in_specs=[SMEM, SMEM] + [VMEM] * 10 + [HBM],
        out_specs=(VMEM, VMEM, VMEM),
        scratch_shapes=[pltpu.SemaphoreType.DMA],
        compiler_params=pltpu.CompilerParams(vmem_limit_bytes=24 << 20),
        name="picked_probes",
    )(times, cos_weights, *own, *other, probe_idx, gaps, left_panel)


def owner_products(parts, probes):
    def kernel(parts_ref, probes_ref, out_ref, held, product, sem):
        fetch = pltpu.make_async_copy(probes_ref, held, sem)
        fetch.start()
        units = parts_ref[:, : CAP * UNIT, :].reshape(GROUP * CAP, TILE // LANES, PART, LANES)
        rows = jnp.concatenate([units[:, n] for n in range(TILE // LANES)], axis=-1).reshape(GROUP * CAP * PART, TILE)
        fetch.wait()
        product[...] = jnp.dot(rows, held[...], preferred_element_type=F32)
        codes = [
            parts_ref[c, CAP * UNIT :, :].astype(F32)[j * (CODE // CAP) : j * (CODE // CAP) + 1, :1]
            for c in range(GROUP)
            for j in range(CAP)
        ]
        for m in range(MB):
            total = jnp.zeros((PART, NPROBE), F32)
            for n, code in enumerate(codes):
                total += jnp.where(code == m, product[n * PART : (n + 1) * PART, :], 0.0)
            turned = total.T.astype(BF16)
            for c in range(NB):
                out_ref[c, :, m * PART : (m + 1) * PART] = turned[c * SET : (c + 1) * SET, :]

    return pl.pallas_call(
        kernel,
        out_shape=jax.ShapeDtypeStruct((NB, SET, MB * PART), BF16),
        in_specs=[VMEM, HBM],
        out_specs=VMEM,
        scratch_shapes=[
            pltpu.VMEM((TILE, NPROBE), BF16),
            pltpu.VMEM((GROUP * CAP * PART, NPROBE), F32),
            pltpu.SemaphoreType.DMA,
        ],
        compiler_params=pltpu.CompilerParams(vmem_limit_bytes=16 << 20),
        name="owner_products",
    )(parts, probes)


def screened_response(parts, first_half, left_panel, weights):
    half = first_half.shape[0]

    def kernel(parts_ref, first_ref, left_ref, weights_ref, out_ref, scaled, second, sem):
        fetch = pltpu.make_async_copy(left_ref.at[pl.ds(half, half), :], second, sem)
        fetch.start()
        core = lax.axis_index("k")
        low = lax.broadcasted_iota(jnp.int32, (SET, LANES), 1) < PART
        for y in range(4):
            held = [
                parts_ref[y, jnp.abs(core - k)].astype(F32) + parts_ref[4 + y, jnp.abs(core - k)].astype(F32)
                for k in range(2)
            ]
            for m in range(MB):
                start = m // 2 * LANES
                both = [held[k][:, start : start + LANES] for k in range(2)]
                turned = 1 - m % 2
                both[turned] = pltpu.roll(both[turned], PART, 1)
                whole = jnp.where(low, both[0], both[1])
                at = (m * 4 + y) * LANES
                for f in range(2):
                    scaled[f * SET : (f + 1) * SET, at : at + LANES] = (
                        whole * weights_ref[f : f + 1, at : at + LANES]
                    ).astype(BF16)
        for n, left in enumerate((first_ref, second)):
            if n == 1:
                fetch.wait()
            product = lax.dot_general(
                scaled[...], left[...], (((1,), (1,)), ((), ())), preferred_element_type=F32
            )
            out_ref[0, :, n * half : (n + 1) * half] = product[:SET]
            out_ref[1, :, n * half : (n + 1) * half] = product[SET:]

    return pl.pallas_call(
        kernel,
        out_shape=jax.ShapeDtypeStruct((2, SET, 2 * half), F32),
        in_specs=[VMEM, VMEM, HBM, VMEM],
        out_specs=VMEM,
        scratch_shapes=[
            pltpu.VMEM((2 * SET, NPAIR), BF16),
            pltpu.VMEM((half, NPAIR), BF16),
            pltpu.SemaphoreType.DMA,
        ],
        compiler_params=pltpu.CompilerParams(vmem_limit_bytes=12 << 20),
        name="screened_response",
    )(parts, first_half, left_panel, weights)


def shards(
    tiles, tile_blocks, tile_pairs, tile_counts, left_panel, gaps, times, cos_weights, bank, probe_idx
):
    stay = lambda array: pltpu.with_memory_space_constraint(array, pltpu.HBM)
    tiles, tile_blocks, tile_pairs, left_panel = map(stay, (tiles, tile_blocks.reshape(SLOTS), tile_pairs, left_panel))
    swap = [(0, 1), (1, 0)]
    with jax.named_scope("parts"):
        owned = [(z, z) for z in range(8)] + [(8 + z, 8 + (z ^ 4)) for z in range(8)]
        bank = lax.ppermute(bank, ("f", "z"), owned)
        parts = outgoing_parts(tiles, tile_blocks, tile_pairs, tile_counts)
        parts = lax.dynamic_update_slice(parts, bank[None, :1, :], (0, ROWS - 1, 0))
        parts = lax.all_to_all(parts, ("k", "u", "z"), 0, 0, tiled=True, axis_index_groups=runs())
    with jax.named_scope("probes"):
        own = [bank] + [lax.ppermute(bank, "y", [(y, (y + n) % 4) for y in range(4)]) for n in (1, 2, 3)]
        other = [lax.ppermute(columns, "k", swap) for columns in own]
        probes, weights, first_half = picked_probes(
            own, other, probe_idx.reshape(1, NPROBE), gaps.reshape(1, NPAIR), times, cos_weights, left_panel
        )
    with jax.named_scope("products"):
        products = owner_products(parts, stay(probes))
        products = lax.all_to_all(products, ("u", "z"), 0, 0, tiled=True)
        product = jnp.sum(products.astype(F32), axis=0).astype(BF16)
    with jax.named_scope("spread"):
        both = jnp.stack([product, lax.ppermute(product, "k", swap)])
        both = lax.all_to_all(jnp.broadcast_to(both, (8,) + both.shape), ("f", "y"), 0, 0, tiled=True)
    with jax.named_scope("response"):
        turned = screened_response(both, first_half, left_panel, weights)
        return jnp.swapaxes(turned, 1, 2)


def solution(mesh):
    fine = Mesh(mesh.devices.reshape(2, 4, 2, 2, 8), ("f", "y", "k", "u", "z"))
    row, col = ("y", "k"), ("u", "z")
    placed = (
        P(col, None, None),
        P(col, None),
        P(col),
        P(col),
        P(row, None),
        P(),
        P(),
        P(),
        P(col, row),
        P(),
    )
    return jax.shard_map(
        shards, mesh=fine, in_specs=placed, out_specs=P("f", row, col), check_vma=False
    )
```

```python
import jax
import jax.numpy as jnp
from jax import lax
from jax.experimental import pallas as pl
from jax.experimental.pallas import tpu as pltpu
from jax.sharding import Mesh, PartitionSpec as P

TILE = 512
MB = 4
CAP = 2
SLOTS = 16
NB = 16
NPAIR = 2048
NPROBE = 512
SET = 32
PART = 64
GROUP = 8
CODE = 16
LANES = 128
UNIT = PART * TILE // LANES
ROWS = CAP * UNIT + CODE
F32 = jnp.float32
BF16 = jnp.bfloat16
SMEM = pl.BlockSpec(memory_space=pltpu.SMEM)
VMEM = pl.BlockSpec(memory_space=pltpu.VMEM)
HBM = pl.BlockSpec(memory_space=pltpu.HBM)


def runs():
    return [[k * 16 + u * 8 + (2 * k + 4 * h + p) % 8 for u in range(2) for p in range(4)] for k in range(2) for h in range(2)]


def outgoing_parts(tiles, blocks, pairs, counts):
    def kernel(blocks_ref, pairs_ref, counts_ref, tiles_ref, out_ref, held, parts, source, sems):
        core = lax.axis_index("k")
        lanes = pl.ds(pl.multiple_of(lax.axis_index("y") * LANES, LANES), LANES)

        def copy(s):
            return pltpu.make_async_copy(tiles_ref.at[s, :, lanes], held.at[s], sems.at[s])

        for s in range(SLOTS):
            copy(s).start()
        live = counts_ref[0]
        far = lax.axis_index("f")
        run = (lax.axis_index("z") + 8 - 2 * core) % 8 // 4
        for d in range(GROUP * CAP):
            source[d] = -1
        for s in range(SLOTS):
            block = blocks_ref[s]
            along = (block % 8 + 14 + 4 * far - 2 * core) % 8
            mine = along // 4 == run
            at = (block // 8 * 4 + along % 4) * CAP
            at = jnp.where(source[at] >= 0, at + 1, at)
            source[at] = jnp.where(jnp.logical_and(s < live, mine), s, source[at])

        wanted = lax.broadcasted_iota(jnp.int32, (PART, LANES), 0) + core * PART
        pick = jnp.where(wanted == lax.broadcasted_iota(jnp.int32, (PART, LANES), 1), 1.0, 0.0).astype(BF16)
        for s in range(SLOTS):
            copy(s).wait()
        for s in range(SLOTS):
            part = lax.dot_general(pick, held[s], (((1,), (1,)), ((), ())), preferred_element_type=F32)
            for n in range(TILE // LANES):
                parts[s, n * PART : (n + 1) * PART, :] = part[:, n * LANES : (n + 1) * LANES].astype(BF16)

        second = lax.broadcasted_iota(jnp.int32, (CODE, LANES), 0) >= CODE // CAP
        for d in range(GROUP):
            codes = []
            for j in range(CAP):
                s = source[d * CAP + j]
                there = jnp.maximum(s, 0)
                full = jnp.where(s >= 0, 1.0, 0.0).astype(BF16)
                out_ref[d, j * UNIT : (j + 1) * UNIT, :] = parts[there] * full
                codes.append(pairs_ref[there].astype(F32))
            out_ref[d, CAP * UNIT :, :] = jnp.where(second, codes[1], codes[0]).astype(BF16)

    return pl.pallas_call(
        kernel,
        out_shape=jax.ShapeDtypeStruct((GROUP, ROWS, LANES), BF16),
        in_specs=[SMEM, SMEM, SMEM, HBM],
        out_specs=VMEM,
        scratch_shapes=[
            pltpu.VMEM((SLOTS, TILE, LANES), BF16),
            pltpu.VMEM((SLOTS, UNIT, LANES), BF16),
            pltpu.SMEM((GROUP * CAP,), jnp.int32),
            pltpu.SemaphoreType.DMA((SLOTS,)),
        ],
        compiler_params=pltpu.CompilerParams(vmem_limit_bytes=8 << 20),
        name="outgoing_parts",
    )(blocks, pairs, counts, tiles)


def after(array, other):
    anywhere = pl.BlockSpec(memory_space=pl.ANY)
    return pl.pallas_call(
        lambda array_ref, other_ref, out_ref: None,
        out_shape=jax.ShapeDtypeStruct(array.shape, array.dtype),
        in_specs=[anywhere, anywhere],
        out_specs=anywhere,
        input_output_aliases={0: 0},
        compiler_params=pltpu.CompilerParams(vmem_limit_bytes=1 << 20),
        name="after",
    )(array, other)


def picked_probes(own, other, probe_idx, gaps, times, cos_weights, left_panel):
    half = left_panel.shape[0] // 2

    def kernel(times_ref, cos_ref, *refs):
        bank_refs, (idx_ref, gaps_ref, left_ref, out_ref, weights_ref, first_ref, sem) = refs[:8], refs[8:]
        fetch = pltpu.make_async_copy(left_ref.at[pl.ds(0, half), :], first_ref, sem)
        fetch.start()
        core, y = lax.axis_index("k"), lax.axis_index("y")
        total = jnp.zeros((TILE, NPROBE), F32)
        for n, bank_ref in enumerate(bank_refs):
            row = (y + 4 - n % 4) % 4 * 2 + (core if n < 4 else 1 - core)
            here = lax.broadcasted_iota(jnp.int32, (LANES, NPROBE), 0) + row * LANES
            pick = jnp.where(here == idx_ref[...], 1.0, 0.0).astype(BF16)
            total += jnp.dot(bank_ref[...], pick, preferred_element_type=F32)
        out_ref[...] = total.astype(BF16)
        first = lax.axis_index("f") * 2
        decays = [jnp.exp(-gaps_ref[...] * times_ref[k]) for k in range(4)]
        for f in range(2):
            weight = decays[0] * cos_ref[first + f, 0]
            for k in range(1, 4):
                weight += decays[k] * cos_ref[first + f, k]
            weights_ref[f : f + 1, :] = weight
        fetch.wait()

    return pl.pallas_call(
        kernel,
        out_shape=(
            jax.ShapeDtypeStruct((TILE, NPROBE), BF16),
            jax.ShapeDtypeStruct((2, NPAIR), F32),
            jax.ShapeDtypeStruct((half, NPAIR), BF16),
        ),
        in_specs=[SMEM, SMEM] + [VMEM] * 10 + [HBM],
        out_specs=(VMEM, VMEM, VMEM),
        scratch_shapes=[pltpu.SemaphoreType.DMA],
        compiler_params=pltpu.CompilerParams(vmem_limit_bytes=24 << 20),
        name="picked_probes",
    )(times, cos_weights, *own, *other, probe_idx, gaps, left_panel)


def owner_products(parts, probes):
    def kernel(parts_ref, probes_ref, out_ref, held, product, sem):
        fetch = pltpu.make_async_copy(probes_ref, held, sem)
        fetch.start()
        units = parts_ref[:, : CAP * UNIT, :].reshape(GROUP * CAP, TILE // LANES, PART, LANES)
        rows = jnp.concatenate([units[:, n] for n in range(TILE // LANES)], axis=-1).reshape(GROUP * CAP * PART, TILE)
        fetch.wait()
        product[...] = jnp.dot(rows, held[...], preferred_element_type=F32)
        codes = [
            parts_ref[c, CAP * UNIT :, :].astype(F32)[j * (CODE // CAP) : j * (CODE // CAP) + 1, :1]
            for c in range(GROUP)
            for j in range(CAP)
        ]
        for m in range(MB):
            total = jnp.zeros((PART, NPROBE), F32)
            for n, code in enumerate(codes):
                total += jnp.where(code == m, product[n * PART : (n + 1) * PART, :], 0.0)
            turned = total.T.astype(BF16)
            for c in range(NB):
                out_ref[c, :, m * PART : (m + 1) * PART] = turned[c * SET : (c + 1) * SET, :]

    return pl.pallas_call(
        kernel,
        out_shape=jax.ShapeDtypeStruct((NB, SET, MB * PART), BF16),
        in_specs=[VMEM, HBM],
        out_specs=VMEM,
        scratch_shapes=[
            pltpu.VMEM((TILE, NPROBE), BF16),
            pltpu.VMEM((GROUP * CAP * PART, NPROBE), F32),
            pltpu.SemaphoreType.DMA,
        ],
        compiler_params=pltpu.CompilerParams(vmem_limit_bytes=16 << 20),
        name="owner_products",
    )(parts, probes)


def screened_response(parts, first_half, left_panel, weights):
    half = first_half.shape[0]

    def kernel(parts_ref, first_ref, left_ref, weights_ref, out_ref, scaled, second, sem):
        fetch = pltpu.make_async_copy(left_ref.at[pl.ds(half, half), :], second, sem)
        fetch.start()
        core = lax.axis_index("k")
        low = lax.broadcasted_iota(jnp.int32, (SET, LANES), 1) < PART
        for y in range(4):
            held = [
                parts_ref[y, jnp.abs(core - k)].astype(F32) + parts_ref[4 + y, jnp.abs(core - k)].astype(F32)
                for k in range(2)
            ]
            for m in range(MB):
                start = m // 2 * LANES
                both = [held[k][:, start : start + LANES] for k in range(2)]
                turned = 1 - m % 2
                both[turned] = pltpu.roll(both[turned], PART, 1)
                whole = jnp.where(low, both[0], both[1])
                at = (m * 4 + y) * LANES
                for f in range(2):
                    scaled[f * SET : (f + 1) * SET, at : at + LANES] = (
                        whole * weights_ref[f : f + 1, at : at + LANES]
                    ).astype(BF16)
        for n, left in enumerate((first_ref, second)):
            if n == 1:
                fetch.wait()
            product = lax.dot_general(
                scaled[...], left[...], (((1,), (1,)), ((), ())), preferred_element_type=F32
            )
            out_ref[0, :, n * half : (n + 1) * half] = product[:SET]
            out_ref[1, :, n * half : (n + 1) * half] = product[SET:]

    return pl.pallas_call(
        kernel,
        out_shape=jax.ShapeDtypeStruct((2, SET, 2 * half), F32),
        in_specs=[VMEM, VMEM, HBM, VMEM],
        out_specs=VMEM,
        scratch_shapes=[
            pltpu.VMEM((2 * SET, NPAIR), BF16),
            pltpu.VMEM((half, NPAIR), BF16),
            pltpu.SemaphoreType.DMA,
        ],
        compiler_params=pltpu.CompilerParams(vmem_limit_bytes=12 << 20),
        name="screened_response",
    )(parts, first_half, left_panel, weights)


def shards(
    tiles, tile_blocks, tile_pairs, tile_counts, left_panel, gaps, times, cos_weights, bank, probe_idx
):
    stay = lambda array: pltpu.with_memory_space_constraint(array, pltpu.HBM)
    tiles, tile_blocks, tile_pairs, left_panel = map(stay, (tiles, tile_blocks.reshape(SLOTS), tile_pairs, left_panel))
    swap = [(0, 1), (1, 0)]
    with jax.named_scope("parts"):
        owned = [(f * 8 + z, f * 8 + (z + 4 * f - 2) % 8) for f in range(2) for z in range(8)]
        bank = lax.ppermute(bank, ("f", "z"), owned)
        parts = outgoing_parts(tiles, tile_blocks, tile_pairs, tile_counts)
        parts = lax.all_to_all(after(parts, bank), ("k", "u", "z"), 0, 0, tiled=True, axis_index_groups=runs())
    with jax.named_scope("probes"):
        own = [bank] + [lax.ppermute(bank, "y", [(y, (y + n) % 4) for y in range(4)]) for n in (1, 2, 3)]
        other = [lax.ppermute(columns, "k", swap) for columns in own]
        probes, weights, first_half = picked_probes(
            own, other, probe_idx.reshape(1, NPROBE), gaps.reshape(1, NPAIR), times, cos_weights, left_panel
        )
    with jax.named_scope("products"):
        products = owner_products(parts, stay(probes))
        products = lax.all_to_all(products, ("u", "z"), 0, 0, tiled=True)
        product = jnp.sum(products.astype(F32), axis=0).astype(BF16)
    with jax.named_scope("spread"):
        both = jnp.stack([product, lax.ppermute(product, "k", swap)])
        both = lax.all_to_all(jnp.broadcast_to(both, (8,) + both.shape), ("f", "y"), 0, 0, tiled=True)
    with jax.named_scope("response"):
        turned = screened_response(both, first_half, left_panel, weights)
        return jnp.swapaxes(turned, 1, 2)


def solution(mesh):
    fine = Mesh(mesh.devices.reshape(2, 4, 2, 2, 8), ("f", "y", "k", "u", "z"))
    row, col = ("y", "k"), ("u", "z")
    placed = (
        P(col, None, None),
        P(col, None),
        P(col),
        P(col),
        P(row, None),
        P(),
        P(),
        P(),
        P(col, row),
        P(),
    )
    return jax.shard_map(
        shards, mesh=fine, in_specs=placed, out_specs=P("f", row, col), check_vma=False
    )
```

```python
import jax
import jax.numpy as jnp
from jax import lax
from jax.experimental import pallas as pl
from jax.experimental.pallas import tpu as pltpu
from jax.sharding import Mesh, PartitionSpec as P

TILE = 512
MB = 4
CAP = 2
SLOTS = 16
NB = 16
NPAIR = 2048
NPROBE = 512
SET = 32
PART = 64
GROUP = 8
CODE = 16
LANES = 128
UNIT = PART * TILE // LANES
ROWS = CAP * UNIT + CODE
F32 = jnp.float32
BF16 = jnp.bfloat16
SMEM = pl.BlockSpec(memory_space=pltpu.SMEM)
VMEM = pl.BlockSpec(memory_space=pltpu.VMEM)
HBM = pl.BlockSpec(memory_space=pltpu.HBM)


def runs():
    return [[k * 16 + u * 8 + (2 * k + 4 * h + p) % 8 for u in range(2) for p in range(4)] for k in range(2) for h in range(2)]


def outgoing_parts(tiles, blocks, pairs, counts):
    def kernel(blocks_ref, pairs_ref, counts_ref, tiles_ref, out_ref, held, parts, source, sems):
        core = lax.axis_index("k")
        lanes = pl.ds(pl.multiple_of(lax.axis_index("y") * LANES, LANES), LANES)

        def copy(s):
            return pltpu.make_async_copy(tiles_ref.at[s, :, lanes], held.at[s], sems.at[s])

        for s in range(SLOTS):
            copy(s).start()
        live = counts_ref[0]
        far = lax.axis_index("f")
        run = (lax.axis_index("z") + 8 - 2 * core) % 8 // 4
        for d in range(GROUP * CAP):
            source[d] = -1
        for s in range(SLOTS):
            block = blocks_ref[s]
            along = (block % 8 + 14 + 4 * far - 2 * core) % 8
            mine = along // 4 == run
            at = (block // 8 * 4 + along % 4) * CAP
            at = jnp.where(source[at] >= 0, at + 1, at)
            source[at] = jnp.where(jnp.logical_and(s < live, mine), s, source[at])

        wanted = lax.broadcasted_iota(jnp.int32, (PART, LANES), 0) + core * PART
        pick = jnp.where(wanted == lax.broadcasted_iota(jnp.int32, (PART, LANES), 1), 1.0, 0.0).astype(BF16)
        for s in range(SLOTS):
            copy(s).wait()
        for s in range(SLOTS):
            part = lax.dot_general(pick, held[s], (((1,), (1,)), ((), ())), preferred_element_type=F32)
            for n in range(TILE // LANES):
                parts[s, n * PART : (n + 1) * PART, :] = part[:, n * LANES : (n + 1) * LANES].astype(BF16)

        second = lax.broadcasted_iota(jnp.int32, (CODE, LANES), 0) >= CODE // CAP
        for d in range(GROUP):
            codes = []
            for j in range(CAP):
                s = source[d * CAP + j]
                there = jnp.maximum(s, 0)
                full = jnp.where(s >= 0, 1.0, 0.0).astype(BF16)
                out_ref[d, j * UNIT : (j + 1) * UNIT, :] = parts[there] * full
                codes.append(pairs_ref[there].astype(F32))
            out_ref[d, CAP * UNIT :, :] = jnp.where(second, codes[1], codes[0]).astype(BF16)

    return pl.pallas_call(
        kernel,
        out_shape=jax.ShapeDtypeStruct((GROUP, ROWS, LANES), BF16),
        in_specs=[SMEM, SMEM, SMEM, HBM],
        out_specs=VMEM,
        scratch_shapes=[
            pltpu.VMEM((SLOTS, TILE, LANES), BF16),
            pltpu.VMEM((SLOTS, UNIT, LANES), BF16),
            pltpu.SMEM((GROUP * CAP,), jnp.int32),
            pltpu.SemaphoreType.DMA((SLOTS,)),
        ],
        compiler_params=pltpu.CompilerParams(vmem_limit_bytes=8 << 20),
        name="outgoing_parts",
    )(blocks, pairs, counts, tiles)


def after(array, other):
    anywhere = pl.BlockSpec(memory_space=pl.ANY)
    return pl.pallas_call(
        lambda array_ref, other_ref, out_ref: None,
        out_shape=jax.ShapeDtypeStruct(array.shape, array.dtype),
        in_specs=[anywhere, anywhere],
        out_specs=anywhere,
        input_output_aliases={0: 0},
        compiler_params=pltpu.CompilerParams(vmem_limit_bytes=1 << 20),
        name="after",
    )(array, other)


def picked_probes(own, other, probe_idx, gaps, times, cos_weights, left_panel):
    cut = left_panel.shape[0] // 8 * 3

    def kernel(times_ref, cos_ref, *refs):
        bank_refs, (idx_ref, gaps_ref, left_ref, out_ref, weights_ref, first_ref, sem) = refs[:8], refs[8:]
        fetch = pltpu.make_async_copy(left_ref.at[pl.ds(0, cut), :], first_ref, sem)
        fetch.start()
        core, y = lax.axis_index("k"), lax.axis_index("y")
        total = jnp.zeros((TILE, NPROBE), F32)
        for n, bank_ref in enumerate(bank_refs):
            row = (y + 4 - n % 4) % 4 * 2 + (core if n < 4 else 1 - core)
            here = lax.broadcasted_iota(jnp.int32, (LANES, NPROBE), 0) + row * LANES
            pick = jnp.where(here == idx_ref[...], 1.0, 0.0).astype(BF16)
            total += jnp.dot(bank_ref[...], pick, preferred_element_type=F32)
        out_ref[...] = total.astype(BF16)
        first = lax.axis_index("f") * 2
        decays = [jnp.exp(-gaps_ref[...] * times_ref[k]) for k in range(4)]
        for f in range(2):
            weight = decays[0] * cos_ref[first + f, 0]
            for k in range(1, 4):
                weight += decays[k] * cos_ref[first + f, k]
            weights_ref[f : f + 1, :] = weight
        fetch.wait()

    return pl.pallas_call(
        kernel,
        out_shape=(
            jax.ShapeDtypeStruct((TILE, NPROBE), BF16),
            jax.ShapeDtypeStruct((2, NPAIR), F32),
            jax.ShapeDtypeStruct((cut, NPAIR), BF16),
        ),
        in_specs=[SMEM, SMEM] + [VMEM] * 10 + [HBM],
        out_specs=(VMEM, VMEM, VMEM),
        scratch_shapes=[pltpu.SemaphoreType.DMA],
        compiler_params=pltpu.CompilerParams(vmem_limit_bytes=24 << 20),
        name="picked_probes",
    )(times, cos_weights, *own, *other, probe_idx, gaps, left_panel)


def owner_products(parts, probes):
    def kernel(parts_ref, probes_ref, out_ref, product):
        units = parts_ref[:, : CAP * UNIT, :].reshape(GROUP * CAP, TILE // LANES, PART, LANES)
        rows = jnp.concatenate([units[:, n] for n in range(TILE // LANES)], axis=-1).reshape(GROUP * CAP * PART, TILE)
        product[...] = jnp.dot(rows, probes_ref[...], preferred_element_type=F32)
        codes = [
            parts_ref[c, CAP * UNIT :, :].astype(F32)[j * (CODE // CAP) : j * (CODE // CAP) + 1, :1]
            for c in range(GROUP)
            for j in range(CAP)
        ]
        for m in range(MB):
            total = jnp.zeros((PART, NPROBE), F32)
            for n, code in enumerate(codes):
                total += jnp.where(code == m, product[n * PART : (n + 1) * PART, :], 0.0)
            turned = total.T.astype(BF16)
            for c in range(NB):
                out_ref[c, :, m * PART : (m + 1) * PART] = turned[c * SET : (c + 1) * SET, :]

    return pl.pallas_call(
        kernel,
        out_shape=jax.ShapeDtypeStruct((NB, SET, MB * PART), BF16),
        in_specs=[VMEM, VMEM],
        out_specs=VMEM,
        scratch_shapes=[pltpu.VMEM((GROUP * CAP * PART, NPROBE), F32)],
        compiler_params=pltpu.CompilerParams(vmem_limit_bytes=16 << 20),
        name="owner_products",
    )(parts, probes)


def screened_response(parts, first, left_panel, weights):
    cut, rows = first.shape[0], left_panel.shape[0]

    def kernel(parts_ref, first_ref, left_ref, weights_ref, out_ref, scaled, second, sem):
        fetch = pltpu.make_async_copy(left_ref.at[pl.ds(cut, rows - cut), :], second, sem)
        fetch.start()
        core = lax.axis_index("k")
        low = lax.broadcasted_iota(jnp.int32, (SET, LANES), 1) < PART
        for y in range(4):
            held = [
                parts_ref[y, jnp.abs(core - k)].astype(F32) + parts_ref[4 + y, jnp.abs(core - k)].astype(F32)
                for k in range(2)
            ]
            for m in range(MB):
                start = m // 2 * LANES
                both = [held[k][:, start : start + LANES] for k in range(2)]
                turned = 1 - m % 2
                both[turned] = pltpu.roll(both[turned], PART, 1)
                whole = jnp.where(low, both[0], both[1])
                at = (m * 4 + y) * LANES
                for f in range(2):
                    scaled[f * SET : (f + 1) * SET, at : at + LANES] = (
                        whole * weights_ref[f : f + 1, at : at + LANES]
                    ).astype(BF16)
        for left, start, stop in ((first_ref, 0, cut), (second, cut, rows)):
            if start == cut:
                fetch.wait()
            product = lax.dot_general(
                scaled[...], left[...], (((1,), (1,)), ((), ())), preferred_element_type=F32
            )
            out_ref[0, :, start:stop] = product[:SET]
            out_ref[1, :, start:stop] = product[SET:]

    return pl.pallas_call(
        kernel,
        out_shape=jax.ShapeDtypeStruct((2, SET, rows), F32),
        in_specs=[VMEM, VMEM, HBM, VMEM],
        out_specs=VMEM,
        scratch_shapes=[
            pltpu.VMEM((2 * SET, NPAIR), BF16),
            pltpu.VMEM((rows - cut, NPAIR), BF16),
            pltpu.SemaphoreType.DMA,
        ],
        compiler_params=pltpu.CompilerParams(vmem_limit_bytes=12 << 20),
        name="screened_response",
    )(parts, first, left_panel, weights)


def shards(
    tiles, tile_blocks, tile_pairs, tile_counts, left_panel, gaps, times, cos_weights, bank, probe_idx
):
    stay = lambda array: pltpu.with_memory_space_constraint(array, pltpu.HBM)
    tiles, tile_blocks, tile_pairs, left_panel = map(stay, (tiles, tile_blocks.reshape(SLOTS), tile_pairs, left_panel))
    swap = [(0, 1), (1, 0)]
    with jax.named_scope("parts"):
        owned = [(f * 8 + z, f * 8 + (z + 4 * f - 2) % 8) for f in range(2) for z in range(8)]
        bank = lax.ppermute(bank, ("f", "z"), owned)
        parts = outgoing_parts(tiles, tile_blocks, tile_pairs, tile_counts)
        parts = lax.all_to_all(after(parts, bank), ("k", "u", "z"), 0, 0, tiled=True, axis_index_groups=runs())
    with jax.named_scope("probes"):
        own = [bank] + [lax.ppermute(bank, "y", [(y, (y + n) % 4) for y in range(4)]) for n in (1, 2, 3)]
        other = [lax.ppermute(columns, "k", swap) for columns in own]
        probes, weights, first = picked_probes(
            own, other, probe_idx.reshape(1, NPROBE), gaps.reshape(1, NPAIR), times, cos_weights, left_panel
        )
    with jax.named_scope("products"):
        products = owner_products(parts, probes)
        products = lax.all_to_all(products, ("u", "z"), 0, 0, tiled=True)
        product = jnp.sum(products.astype(F32), axis=0).astype(BF16)
    with jax.named_scope("spread"):
        both = jnp.stack([product, lax.ppermute(product, "k", swap)])
        both = lax.all_to_all(jnp.broadcast_to(both, (8,) + both.shape), ("f", "y"), 0, 0, tiled=True)
    with jax.named_scope("response"):
        turned = screened_response(both, first, left_panel, weights)
        return jnp.swapaxes(turned, 1, 2)


def solution(mesh):
    fine = Mesh(mesh.devices.reshape(2, 4, 2, 2, 8), ("f", "y", "k", "u", "z"))
    row, col = ("y", "k"), ("u", "z")
    placed = (
        P(col, None, None),
        P(col, None),
        P(col),
        P(col),
        P(row, None),
        P(),
        P(),
        P(),
        P(col, row),
        P(),
    )
    return jax.shard_map(
        shards, mesh=fine, in_specs=placed, out_specs=P("f", row, col), check_vma=False
    )
```

```python
import jax
import jax.numpy as jnp
from jax import lax
from jax.experimental import pallas as pl
from jax.experimental.pallas import tpu as pltpu
from jax.sharding import Mesh, PartitionSpec as P

TILE = 512
MB = 4
CAP = 2
SLOTS = 16
NB = 16
NPAIR = 2048
NPROBE = 512
SET = 32
PART = 64
GROUP = 8
CODE = 16
LANES = 128
UNIT = PART * TILE // LANES
ROWS = CAP * UNIT + CODE
F32 = jnp.float32
BF16 = jnp.bfloat16
SMEM = pl.BlockSpec(memory_space=pltpu.SMEM)
VMEM = pl.BlockSpec(memory_space=pltpu.VMEM)
HBM = pl.BlockSpec(memory_space=pltpu.HBM)


def runs():
    return [[k * 16 + u * 8 + (2 * k + 4 * h + p) % 8 for u in range(2) for p in range(4)] for k in range(2) for h in range(2)]


def outgoing_parts(tiles, blocks, pairs, counts):
    def kernel(blocks_ref, pairs_ref, counts_ref, tiles_ref, out_ref, held, source, sems):
        core = lax.axis_index("k")
        lanes = pl.ds(pl.multiple_of(lax.axis_index("y") * LANES, LANES), LANES)

        def copy(s):
            return pltpu.make_async_copy(tiles_ref.at[s, :, lanes], held.at[s], sems.at[s])

        for s in range(SLOTS):
            copy(s).start()
        live = counts_ref[0]
        far = lax.axis_index("f")
        run = (lax.axis_index("z") + 8 - 2 * core) % 8 // 4
        for d in range(GROUP * CAP):
            source[d] = -1
        for s in range(SLOTS):
            block = blocks_ref[s]
            along = (block % 8 + 14 + 4 * far - 2 * core) % 8
            mine = along // 4 == run
            at = (block // 8 * 4 + along % 4) * CAP
            at = jnp.where(source[at] >= 0, at + 1, at)
            source[at] = jnp.where(jnp.logical_and(s < live, mine), s, source[at])

        wanted = lax.broadcasted_iota(jnp.int32, (PART, LANES), 0) + core * PART
        pick = jnp.where(wanted == lax.broadcasted_iota(jnp.int32, (PART, LANES), 1), 1.0, 0.0).astype(BF16)
        for s in range(SLOTS):
            copy(s).wait()
        second = lax.broadcasted_iota(jnp.int32, (CODE, LANES), 0) >= CODE // CAP
        for d in range(GROUP):
            codes = []
            for j in range(CAP):
                s = source[d * CAP + j]
                there = jnp.maximum(s, 0)
                full = jnp.where(s >= 0, 1.0, 0.0)
                part = lax.dot_general(pick, held[there], (((1,), (1,)), ((), ())), preferred_element_type=F32) * full
                for n in range(TILE // LANES):
                    start = j * UNIT + n * PART
                    out_ref[d, start : start + PART, :] = part[:, n * LANES : (n + 1) * LANES].astype(BF16)
                codes.append(pairs_ref[there].astype(F32))
            out_ref[d, CAP * UNIT :, :] = jnp.where(second, codes[1], codes[0]).astype(BF16)

    return pl.pallas_call(
        kernel,
        out_shape=jax.ShapeDtypeStruct((GROUP, ROWS, LANES), BF16),
        in_specs=[SMEM, SMEM, SMEM, HBM],
        out_specs=VMEM,
        scratch_shapes=[
            pltpu.VMEM((SLOTS, TILE, LANES), BF16),
            pltpu.SMEM((GROUP * CAP,), jnp.int32),
            pltpu.SemaphoreType.DMA((SLOTS,)),
        ],
        compiler_params=pltpu.CompilerParams(vmem_limit_bytes=8 << 20),
        name="outgoing_parts",
    )(blocks, pairs, counts, tiles)


def after(array, other):
    anywhere = pl.BlockSpec(memory_space=pl.ANY)
    return pl.pallas_call(
        lambda array_ref, other_ref, out_ref: None,
        out_shape=jax.ShapeDtypeStruct(array.shape, array.dtype),
        in_specs=[anywhere, anywhere],
        out_specs=anywhere,
        input_output_aliases={0: 0},
        compiler_params=pltpu.CompilerParams(vmem_limit_bytes=1 << 20),
        name="after",
    )(array, other)


def picked_probes(own, other, probe_idx, gaps, times, cos_weights, left_panel):
    cut = left_panel.shape[0] // 8 * 3

    def kernel(times_ref, cos_ref, *refs):
        bank_refs, (idx_ref, gaps_ref, left_ref, out_ref, weights_ref, first_ref, sem) = refs[:8], refs[8:]
        fetch = pltpu.make_async_copy(left_ref.at[pl.ds(0, cut), :], first_ref, sem)
        fetch.start()
        core, y = lax.axis_index("k"), lax.axis_index("y")
        total = jnp.zeros((TILE, NPROBE), F32)
        for n, bank_ref in enumerate(bank_refs):
            row = (y + 4 - n % 4) % 4 * 2 + (core if n < 4 else 1 - core)
            here = lax.broadcasted_iota(jnp.int32, (LANES, NPROBE), 0) + row * LANES
            pick = jnp.where(here == idx_ref[...], 1.0, 0.0).astype(BF16)
            total += jnp.dot(bank_ref[...], pick, preferred_element_type=F32)
        out_ref[...] = total.astype(BF16)
        first = lax.axis_index("f") * 2
        decays = [jnp.exp(-gaps_ref[...] * times_ref[k]) for k in range(4)]
        for f in range(2):
            weight = decays[0] * cos_ref[first + f, 0]
            for k in range(1, 4):
                weight += decays[k] * cos_ref[first + f, k]
            weights_ref[f : f + 1, :] = weight
        fetch.wait()

    return pl.pallas_call(
        kernel,
        out_shape=(
            jax.ShapeDtypeStruct((TILE, NPROBE), BF16),
            jax.ShapeDtypeStruct((2, NPAIR), F32),
            jax.ShapeDtypeStruct((cut, NPAIR), BF16),
        ),
        in_specs=[SMEM, SMEM] + [VMEM] * 10 + [HBM],
        out_specs=(VMEM, VMEM, VMEM),
        scratch_shapes=[pltpu.SemaphoreType.DMA],
        compiler_params=pltpu.CompilerParams(vmem_limit_bytes=24 << 20),
        name="picked_probes",
    )(times, cos_weights, *own, *other, probe_idx, gaps, left_panel)


def owner_products(parts, probes):
    def kernel(parts_ref, probes_ref, out_ref, product):
        units = parts_ref[:, : CAP * UNIT, :].reshape(GROUP * CAP, TILE // LANES, PART, LANES)
        rows = jnp.concatenate([units[:, n] for n in range(TILE // LANES)], axis=-1).reshape(GROUP * CAP * PART, TILE)
        product[...] = jnp.dot(rows, probes_ref[...], preferred_element_type=F32)
        codes = [
            parts_ref[c, CAP * UNIT :, :].astype(F32)[j * (CODE // CAP) : j * (CODE // CAP) + 1, :1]
            for c in range(GROUP)
            for j in range(CAP)
        ]
        for m in range(MB):
            total = jnp.zeros((PART, NPROBE), F32)
            for n, code in enumerate(codes):
                total += jnp.where(code == m, product[n * PART : (n + 1) * PART, :], 0.0)
            turned = total.T.astype(BF16)
            for c in range(NB):
                out_ref[c, :, m * PART : (m + 1) * PART] = turned[c * SET : (c + 1) * SET, :]

    return pl.pallas_call(
        kernel,
        out_shape=jax.ShapeDtypeStruct((NB, SET, MB * PART), BF16),
        in_specs=[VMEM, VMEM],
        out_specs=VMEM,
        scratch_shapes=[pltpu.VMEM((GROUP * CAP * PART, NPROBE), F32)],
        compiler_params=pltpu.CompilerParams(vmem_limit_bytes=16 << 20),
        name="owner_products",
    )(parts, probes)


def screened_response(parts, first, left_panel, weights):
    cut, rows = first.shape[0], left_panel.shape[0]

    def kernel(parts_ref, first_ref, left_ref, weights_ref, out_ref, scaled, second, sem):
        fetch = pltpu.make_async_copy(left_ref.at[pl.ds(cut, rows - cut), :], second, sem)
        fetch.start()
        core = lax.axis_index("k")
        low = lax.broadcasted_iota(jnp.int32, (SET, LANES), 1) < PART
        for y in range(4):
            held = [
                parts_ref[y, jnp.abs(core - k)].astype(F32) + parts_ref[4 + y, jnp.abs(core - k)].astype(F32)
                for k in range(2)
            ]
            for m in range(MB):
                start = m // 2 * LANES
                both = [held[k][:, start : start + LANES] for k in range(2)]
                turned = 1 - m % 2
                both[turned] = pltpu.roll(both[turned], PART, 1)
                whole = jnp.where(low, both[0], both[1])
                at = (m * 4 + y) * LANES
                for f in range(2):
                    scaled[f * SET : (f + 1) * SET, at : at + LANES] = (
                        whole * weights_ref[f : f + 1, at : at + LANES]
                    ).astype(BF16)
        for left, start, stop in ((first_ref, 0, cut), (second, cut, rows)):
            if start == cut:
                fetch.wait()
            product = lax.dot_general(
                scaled[...], left[...], (((1,), (1,)), ((), ())), preferred_element_type=F32
            )
            out_ref[0, :, start:stop] = product[:SET]
            out_ref[1, :, start:stop] = product[SET:]

    return pl.pallas_call(
        kernel,
        out_shape=jax.ShapeDtypeStruct((2, SET, rows), F32),
        in_specs=[VMEM, VMEM, HBM, VMEM],
        out_specs=VMEM,
        scratch_shapes=[
            pltpu.VMEM((2 * SET, NPAIR), BF16),
            pltpu.VMEM((rows - cut, NPAIR), BF16),
            pltpu.SemaphoreType.DMA,
        ],
        compiler_params=pltpu.CompilerParams(vmem_limit_bytes=12 << 20),
        name="screened_response",
    )(parts, first, left_panel, weights)


def shards(
    tiles, tile_blocks, tile_pairs, tile_counts, left_panel, gaps, times, cos_weights, bank, probe_idx
):
    stay = lambda array: pltpu.with_memory_space_constraint(array, pltpu.HBM)
    tiles, tile_blocks, tile_pairs, left_panel = map(stay, (tiles, tile_blocks.reshape(SLOTS), tile_pairs, left_panel))
    swap = [(0, 1), (1, 0)]
    with jax.named_scope("parts"):
        owned = [(f * 8 + z, f * 8 + (z + 4 * f - 2) % 8) for f in range(2) for z in range(8)]
        bank = lax.ppermute(bank, ("f", "z"), owned)
        parts = outgoing_parts(tiles, tile_blocks, tile_pairs, tile_counts)
        parts = lax.all_to_all(after(parts, bank), ("k", "u", "z"), 0, 0, tiled=True, axis_index_groups=runs())
    with jax.named_scope("probes"):
        own = [bank] + [lax.ppermute(bank, "y", [(y, (y + n) % 4) for y in range(4)]) for n in (1, 2, 3)]
        other = [lax.ppermute(columns, "k", swap) for columns in own]
        probes, weights, first = picked_probes(
            own, other, probe_idx.reshape(1, NPROBE), gaps.reshape(1, NPAIR), times, cos_weights, left_panel
        )
    with jax.named_scope("products"):
        products = owner_products(parts, probes)
        products = lax.all_to_all(products, ("u", "z"), 0, 0, tiled=True)
        product = jnp.sum(products.astype(F32), axis=0).astype(BF16)
    with jax.named_scope("spread"):
        both = jnp.stack([product, lax.ppermute(product, "k", swap)])
        both = lax.all_to_all(jnp.broadcast_to(both, (8,) + both.shape), ("f", "y"), 0, 0, tiled=True)
    with jax.named_scope("response"):
        turned = screened_response(both, first, left_panel, weights)
        return jnp.swapaxes(turned, 1, 2)


def solution(mesh):
    fine = Mesh(mesh.devices.reshape(2, 4, 2, 2, 8), ("f", "y", "k", "u", "z"))
    row, col = ("y", "k"), ("u", "z")
    placed = (
        P(col, None, None),
        P(col, None),
        P(col),
        P(col),
        P(row, None),
        P(),
        P(),
        P(),
        P(col, row),
        P(),
    )
    return jax.shard_map(
        shards, mesh=fine, in_specs=placed, out_specs=P("f", row, col), check_vma=False
    )
```

```python
import jax
import jax.numpy as jnp
from jax import lax
from jax.experimental import pallas as pl
from jax.experimental.pallas import tpu as pltpu
from jax.sharding import Mesh, PartitionSpec as P

TILE = 512
MB = 4
CAP = 2
SLOTS = 16
NB = 16
NPAIR = 2048
NPROBE = 512
SET = 32
PART = 64
GROUP = 8
CODE = 16
LANES = 128
UNIT = PART * TILE // LANES
ROWS = CAP * UNIT + CODE
F32 = jnp.float32
BF16 = jnp.bfloat16
SMEM = pl.BlockSpec(memory_space=pltpu.SMEM)
VMEM = pl.BlockSpec(memory_space=pltpu.VMEM)
HBM = pl.BlockSpec(memory_space=pltpu.HBM)


def runs():
    return [[k * 16 + u * 8 + (2 * k + 4 * h + p) % 8 for u in range(2) for p in range(4)] for k in range(2) for h in range(2)]


def outgoing_parts(tiles, blocks, pairs, counts):
    def kernel(blocks_ref, pairs_ref, counts_ref, tiles_ref, out_ref, held, parts, source, sems):
        core = lax.axis_index("k")
        lanes = pl.ds(pl.multiple_of(lax.axis_index("y") * LANES, LANES), LANES)

        def copy(s):
            return pltpu.make_async_copy(tiles_ref.at[s, :, lanes], held.at[s], sems.at[s])

        for s in range(SLOTS):
            copy(s).start()
        live = counts_ref[0]
        far = lax.axis_index("f")
        run = (lax.axis_index("z") + 8 - 2 * core) % 8 // 4
        for d in range(GROUP * CAP):
            source[d] = -1
        for s in range(SLOTS):
            block = blocks_ref[s]
            along = (block % 8 + 14 + 4 * far - 2 * core) % 8
            mine = along // 4 == run
            at = (block // 8 * 4 + along % 4) * CAP
            at = jnp.where(source[at] >= 0, at + 1, at)
            source[at] = jnp.where(jnp.logical_and(s < live, mine), s, source[at])

        wanted = lax.broadcasted_iota(jnp.int32, (PART, LANES), 0) + core * PART
        pick = jnp.where(wanted == lax.broadcasted_iota(jnp.int32, (PART, LANES), 1), 1.0, 0.0).astype(BF16)
        for s in range(SLOTS):
            copy(s).wait()
        for s in range(SLOTS):
            part = lax.dot_general(pick, held[s], (((1,), (1,)), ((), ())), preferred_element_type=F32)
            for n in range(TILE // LANES):
                parts[s, n * PART : (n + 1) * PART, :] = part[:, n * LANES : (n + 1) * LANES].astype(BF16)

        second = lax.broadcasted_iota(jnp.int32, (CODE, LANES), 0) >= CODE // CAP
        for d in range(GROUP):
            codes = []
            for j in range(CAP):
                s = source[d * CAP + j]
                there = jnp.maximum(s, 0)
                full = jnp.where(s >= 0, 1.0, 0.0).astype(BF16)
                out_ref[d, j * UNIT : (j + 1) * UNIT, :] = parts[there] * full
                codes.append(pairs_ref[there].astype(F32))
            out_ref[d, CAP * UNIT :, :] = jnp.where(second, codes[1], codes[0]).astype(BF16)

    return pl.pallas_call(
        kernel,
        out_shape=jax.ShapeDtypeStruct((GROUP, ROWS, LANES), BF16),
        in_specs=[SMEM, SMEM, SMEM, HBM],
        out_specs=VMEM,
        scratch_shapes=[
            pltpu.VMEM((SLOTS, TILE, LANES), BF16),
            pltpu.VMEM((SLOTS, UNIT, LANES), BF16),
            pltpu.SMEM((GROUP * CAP,), jnp.int32),
            pltpu.SemaphoreType.DMA((SLOTS,)),
        ],
        compiler_params=pltpu.CompilerParams(vmem_limit_bytes=8 << 20),
        name="outgoing_parts",
    )(blocks, pairs, counts, tiles)


def after(array, other):
    anywhere = pl.BlockSpec(memory_space=pl.ANY)
    return pl.pallas_call(
        lambda array_ref, other_ref, out_ref: None,
        out_shape=jax.ShapeDtypeStruct(array.shape, array.dtype),
        in_specs=[anywhere, anywhere],
        out_specs=anywhere,
        input_output_aliases={0: 0},
        compiler_params=pltpu.CompilerParams(vmem_limit_bytes=1 << 20),
        name="after",
    )(array, other)


def picked_probes(own, other, probe_idx, gaps, times, cos_weights, left_panel):
    cut = left_panel.shape[0] // 8 * 3

    def kernel(times_ref, cos_ref, *refs):
        bank_refs, (idx_ref, gaps_ref, left_ref, out_ref, weights_ref, first_ref, sem) = refs[:8], refs[8:]
        fetch = pltpu.make_async_copy(left_ref.at[pl.ds(0, cut), :], first_ref, sem)
        fetch.start()
        core, y = lax.axis_index("k"), lax.axis_index("y")
        total = jnp.zeros((TILE, NPROBE), F32)
        for n, bank_ref in enumerate(bank_refs):
            row = (y + 4 - n % 4) % 4 * 2 + (core if n < 4 else 1 - core)
            here = lax.broadcasted_iota(jnp.int32, (LANES, NPROBE), 0) + row * LANES
            pick = jnp.where(here == idx_ref[...], 1.0, 0.0).astype(BF16)
            total += jnp.dot(bank_ref[...], pick, preferred_element_type=F32)
        out_ref[...] = total.astype(BF16)
        first = lax.axis_index("f") * 2
        decays = [jnp.exp(-gaps_ref[...] * times_ref[k]) for k in range(4)]
        for f in range(2):
            weight = decays[0] * cos_ref[first + f, 0]
            for k in range(1, 4):
                weight += decays[k] * cos_ref[first + f, k]
            weights_ref[f : f + 1, :] = weight
        fetch.wait()

    return pl.pallas_call(
        kernel,
        out_shape=(
            jax.ShapeDtypeStruct((TILE, NPROBE), BF16),
            jax.ShapeDtypeStruct((2, NPAIR), F32),
            jax.ShapeDtypeStruct((cut, NPAIR), BF16),
        ),
        in_specs=[SMEM, SMEM] + [VMEM] * 10 + [HBM],
        out_specs=(VMEM, VMEM, VMEM),
        scratch_shapes=[pltpu.SemaphoreType.DMA],
        compiler_params=pltpu.CompilerParams(vmem_limit_bytes=24 << 20),
        name="picked_probes",
    )(times, cos_weights, *own, *other, probe_idx, gaps, left_panel)


def owner_products(parts, probes):
    def kernel(parts_ref, probes_ref, out_ref, product):
        units = parts_ref[:, : CAP * UNIT, :].reshape(GROUP * CAP, TILE // LANES, PART, LANES)
        rows = jnp.concatenate([units[:, n] for n in range(TILE // LANES)], axis=-1).reshape(GROUP * CAP * PART, TILE)
        product[...] = jnp.dot(rows, probes_ref[...], preferred_element_type=F32)
        codes = [
            parts_ref[c, CAP * UNIT :, :].astype(F32)[j * (CODE // CAP) : j * (CODE // CAP) + 1, :1]
            for c in range(GROUP)
            for j in range(CAP)
        ]
        for m in range(MB):
            total = jnp.zeros((PART, NPROBE), F32)
            for n, code in enumerate(codes):
                total += jnp.where(code == m, product[n * PART : (n + 1) * PART, :], 0.0)
            turned = total.T.astype(BF16)
            for c in range(NB):
                out_ref[c, :, m * PART : (m + 1) * PART] = turned[c * SET : (c + 1) * SET, :]

    return pl.pallas_call(
        kernel,
        out_shape=jax.ShapeDtypeStruct((NB, SET, MB * PART), BF16),
        in_specs=[VMEM, VMEM],
        out_specs=VMEM,
        scratch_shapes=[pltpu.VMEM((GROUP * CAP * PART, NPROBE), F32)],
        compiler_params=pltpu.CompilerParams(vmem_limit_bytes=16 << 20),
        name="owner_products",
    )(parts, probes)


def screened_response(parts, first, left_panel, weights):
    cut, rows = first.shape[0], left_panel.shape[0]

    def kernel(*refs):
        part_refs, (first_ref, left_ref, weights_ref, out_ref, scaled, second, sem) = refs[:4], refs[4:]
        fetch = pltpu.make_async_copy(left_ref.at[pl.ds(cut, rows - cut), :], second, sem)
        fetch.start()
        core = lax.axis_index("k")
        low = lax.broadcasted_iota(jnp.int32, (SET, LANES), 1) < PART
        for n, part_ref in enumerate(part_refs):
            y = (lax.axis_index("y") + 4 - n) % 4
            held = [part_ref[jnp.abs(core - k)].astype(F32) for k in range(2)]
            for m in range(MB):
                start = m // 2 * LANES
                both = [held[k][:, start : start + LANES] for k in range(2)]
                turned = 1 - m % 2
                both[turned] = pltpu.roll(both[turned], PART, 1)
                whole = jnp.where(low, both[0], both[1])
                at = pl.ds(pl.multiple_of((m * 4 + y) * LANES, LANES), LANES)
                for f in range(2):
                    scaled[f * SET : (f + 1) * SET, at] = (whole * weights_ref[f : f + 1, at]).astype(BF16)
        for left, start, stop in ((first_ref, 0, cut), (second, cut, rows)):
            if start == cut:
                fetch.wait()
            product = lax.dot_general(
                scaled[...], left[...], (((1,), (1,)), ((), ())), preferred_element_type=F32
            )
            out_ref[0, :, start:stop] = product[:SET]
            out_ref[1, :, start:stop] = product[SET:]

    return pl.pallas_call(
        kernel,
        out_shape=jax.ShapeDtypeStruct((2, SET, rows), F32),
        in_specs=[VMEM] * 5 + [HBM, VMEM],
        out_specs=VMEM,
        scratch_shapes=[
            pltpu.VMEM((2 * SET, NPAIR), BF16),
            pltpu.VMEM((rows - cut, NPAIR), BF16),
            pltpu.SemaphoreType.DMA,
        ],
        compiler_params=pltpu.CompilerParams(vmem_limit_bytes=12 << 20),
        name="screened_response",
    )(*parts, first, left_panel, weights)


def shards(
    tiles, tile_blocks, tile_pairs, tile_counts, left_panel, gaps, times, cos_weights, bank, probe_idx
):
    stay = lambda array: pltpu.with_memory_space_constraint(array, pltpu.HBM)
    tiles, tile_blocks, tile_pairs, left_panel = map(stay, (tiles, tile_blocks.reshape(SLOTS), tile_pairs, left_panel))
    swap = [(0, 1), (1, 0)]
    with jax.named_scope("parts"):
        owned = [(f * 8 + z, f * 8 + (z + 4 * f - 2) % 8) for f in range(2) for z in range(8)]
        bank = lax.ppermute(bank, ("f", "z"), owned)
        parts = outgoing_parts(tiles, tile_blocks, tile_pairs, tile_counts)
        parts = lax.all_to_all(after(parts, bank), ("k", "u", "z"), 0, 0, tiled=True, axis_index_groups=runs())
    with jax.named_scope("probes"):
        own = [bank] + [lax.ppermute(bank, "y", [(y, (y + n) % 4) for y in range(4)]) for n in (1, 2, 3)]
        other = [lax.ppermute(columns, "k", swap) for columns in own]
        probes, weights, first = picked_probes(
            own, other, probe_idx.reshape(1, NPROBE), gaps.reshape(1, NPAIR), times, cos_weights, left_panel
        )
    with jax.named_scope("products"):
        products = owner_products(parts, probes)
        products = lax.all_to_all(products, ("u", "z"), 0, 0, tiled=True)
        product = jnp.sum(products.astype(F32), axis=0).astype(BF16)
    with jax.named_scope("spread"):
        product = (product.astype(F32) + lax.ppermute(product, "f", swap).astype(F32)).astype(BF16)
        both = jnp.stack([product, lax.ppermute(product, "k", swap)])
        both = [both] + [lax.ppermute(both, "y", [(y, (y + n) % 4) for y in range(4)]) for n in (1, 2, 3)]
    with jax.named_scope("response"):
        turned = screened_response(both, first, left_panel, weights)
        return jnp.swapaxes(turned, 1, 2)


def solution(mesh):
    fine = Mesh(mesh.devices.reshape(2, 4, 2, 2, 8), ("f", "y", "k", "u", "z"))
    row, col = ("y", "k"), ("u", "z")
    placed = (
        P(col, None, None),
        P(col, None),
        P(col),
        P(col),
        P(row, None),
        P(),
        P(),
        P(),
        P(col, row),
        P(),
    )
    return jax.shard_map(
        shards, mesh=fine, in_specs=placed, out_specs=P("f", row, col), check_vma=False
    )
```

```python
import jax
import jax.numpy as jnp
from jax import lax
from jax.experimental import pallas as pl
from jax.experimental.pallas import tpu as pltpu
from jax.sharding import Mesh, PartitionSpec as P

TILE = 512
MB = 4
CAP = 2
SLOTS = 16
NB = 16
NPAIR = 2048
NPROBE = 512
SET = 32
PART = 64
GROUP = 8
CODE = 16
LANES = 128
UNIT = PART * TILE // LANES
ROWS = CAP * UNIT + CODE
F32 = jnp.float32
BF16 = jnp.bfloat16
SMEM = pl.BlockSpec(memory_space=pltpu.SMEM)
VMEM = pl.BlockSpec(memory_space=pltpu.VMEM)
HBM = pl.BlockSpec(memory_space=pltpu.HBM)


def runs():
    return [[k * 16 + u * 8 + (2 * k + 4 * h + p) % 8 for u in range(2) for p in range(4)] for k in range(2) for h in range(2)]


def outgoing_parts(tiles, blocks, pairs, counts):
    def kernel(blocks_ref, pairs_ref, counts_ref, tiles_ref, out_ref, held, parts, source, sems):
        core = lax.axis_index("k")
        lanes = pl.ds(pl.multiple_of(lax.axis_index("y") * LANES, LANES), LANES)

        def copy(s):
            return pltpu.make_async_copy(tiles_ref.at[s, :, lanes], held.at[s], sems.at[s])

        for s in range(SLOTS):
            copy(s).start()
        live = counts_ref[0]
        far = lax.axis_index("f")
        run = (lax.axis_index("z") + 8 - 2 * core) % 8 // 4
        for d in range(GROUP * CAP):
            source[d] = -1
        for s in range(SLOTS):
            block = blocks_ref[s]
            along = (block % 8 + 14 + 4 * far - 2 * core) % 8
            mine = along // 4 == run
            at = (block // 8 * 4 + along % 4) * CAP
            at = jnp.where(source[at] >= 0, at + 1, at)
            source[at] = jnp.where(jnp.logical_and(s < live, mine), s, source[at])

        wanted = lax.broadcasted_iota(jnp.int32, (PART, LANES), 0) + core * PART
        pick = jnp.where(wanted == lax.broadcasted_iota(jnp.int32, (PART, LANES), 1), 1.0, 0.0).astype(BF16)
        for s in range(SLOTS):
            copy(s).wait()
        for s in range(SLOTS):
            part = lax.dot_general(pick, held[s], (((1,), (1,)), ((), ())), preferred_element_type=F32)
            for n in range(TILE // LANES):
                parts[s, n * PART : (n + 1) * PART, :] = part[:, n * LANES : (n + 1) * LANES].astype(BF16)

        second = lax.broadcasted_iota(jnp.int32, (CODE, LANES), 0) >= CODE // CAP
        for d in range(GROUP):
            codes = []
            for j in range(CAP):
                s = source[d * CAP + j]
                there = jnp.maximum(s, 0)
                full = jnp.where(s >= 0, 1.0, 0.0).astype(BF16)
                out_ref[d, j * UNIT : (j + 1) * UNIT, :] = parts[there] * full
                codes.append(pairs_ref[there].astype(F32))
            out_ref[d, CAP * UNIT :, :] = jnp.where(second, codes[1], codes[0]).astype(BF16)

    return pl.pallas_call(
        kernel,
        out_shape=jax.ShapeDtypeStruct((GROUP, ROWS, LANES), BF16),
        in_specs=[SMEM, SMEM, SMEM, HBM],
        out_specs=VMEM,
        scratch_shapes=[
            pltpu.VMEM((SLOTS, TILE, LANES), BF16),
            pltpu.VMEM((SLOTS, UNIT, LANES), BF16),
            pltpu.SMEM((GROUP * CAP,), jnp.int32),
            pltpu.SemaphoreType.DMA((SLOTS,)),
        ],
        compiler_params=pltpu.CompilerParams(vmem_limit_bytes=8 << 20),
        name="outgoing_parts",
    )(blocks, pairs, counts, tiles)


def after(array, other):
    anywhere = pl.BlockSpec(memory_space=pl.ANY)
    return pl.pallas_call(
        lambda array_ref, other_ref, out_ref: None,
        out_shape=jax.ShapeDtypeStruct(array.shape, array.dtype),
        in_specs=[anywhere, anywhere],
        out_specs=anywhere,
        input_output_aliases={0: 0},
        compiler_params=pltpu.CompilerParams(vmem_limit_bytes=1 << 20),
        name="after",
    )(array, other)


def picked_probes(own, other, probe_idx, gaps, times, cos_weights, left_panel):
    cut = left_panel.shape[0] // 16 * 7

    def kernel(times_ref, cos_ref, *refs):
        bank_refs, (idx_ref, gaps_ref, left_ref, out_ref, weights_ref, first_ref, sem) = refs[:8], refs[8:]
        fetch = pltpu.make_async_copy(left_ref.at[pl.ds(0, cut), :], first_ref, sem)
        fetch.start()
        core, y = lax.axis_index("k"), lax.axis_index("y")
        total = jnp.zeros((TILE, NPROBE), F32)
        for n, bank_ref in enumerate(bank_refs):
            row = (y + 4 - n % 4) % 4 * 2 + (core if n < 4 else 1 - core)
            here = lax.broadcasted_iota(jnp.int32, (LANES, NPROBE), 0) + row * LANES
            pick = jnp.where(here == idx_ref[...], 1.0, 0.0).astype(BF16)
            total += jnp.dot(bank_ref[...], pick, preferred_element_type=F32)
        out_ref[...] = total.astype(BF16)
        first = lax.axis_index("f") * 2
        decays = [jnp.exp(-gaps_ref[...] * times_ref[k]) for k in range(4)]
        for f in range(2):
            weight = decays[0] * cos_ref[first + f, 0]
            for k in range(1, 4):
                weight += decays[k] * cos_ref[first + f, k]
            weights_ref[f : f + 1, :] = weight
        fetch.wait()

    return pl.pallas_call(
        kernel,
        out_shape=(
            jax.ShapeDtypeStruct((TILE, NPROBE), BF16),
            jax.ShapeDtypeStruct((2, NPAIR), F32),
            jax.ShapeDtypeStruct((cut, NPAIR), BF16),
        ),
        in_specs=[SMEM, SMEM] + [VMEM] * 10 + [HBM],
        out_specs=(VMEM, VMEM, VMEM),
        scratch_shapes=[pltpu.SemaphoreType.DMA],
        compiler_params=pltpu.CompilerParams(vmem_limit_bytes=24 << 20),
        name="picked_probes",
    )(times, cos_weights, *own, *other, probe_idx, gaps, left_panel)


def owner_products(parts, probes):
    def kernel(parts_ref, probes_ref, out_ref, product):
        units = parts_ref[:, : CAP * UNIT, :].reshape(GROUP * CAP, TILE // LANES, PART, LANES)
        rows = jnp.concatenate([units[:, n] for n in range(TILE // LANES)], axis=-1).reshape(GROUP * CAP * PART, TILE)
        product[...] = jnp.dot(rows, probes_ref[...], preferred_element_type=F32)
        codes = [
            parts_ref[c, CAP * UNIT :, :].astype(F32)[j * (CODE // CAP) : j * (CODE // CAP) + 1, :1]
            for c in range(GROUP)
            for j in range(CAP)
        ]
        for m in range(MB):
            total = jnp.zeros((PART, NPROBE), F32)
            for n, code in enumerate(codes):
                total += jnp.where(code == m, product[n * PART : (n + 1) * PART, :], 0.0)
            turned = total.T.astype(BF16)
            for c in range(NB):
                out_ref[c, :, m * PART : (m + 1) * PART] = turned[c * SET : (c + 1) * SET, :]

    return pl.pallas_call(
        kernel,
        out_shape=jax.ShapeDtypeStruct((NB, SET, MB * PART), BF16),
        in_specs=[VMEM, VMEM],
        out_specs=VMEM,
        scratch_shapes=[pltpu.VMEM((GROUP * CAP * PART, NPROBE), F32)],
        compiler_params=pltpu.CompilerParams(vmem_limit_bytes=16 << 20),
        name="owner_products",
    )(parts, probes)


def screened_response(parts, first, left_panel, weights):
    cut, rows = first.shape[0], left_panel.shape[0]

    def kernel(parts_ref, first_ref, left_ref, weights_ref, out_ref, scaled, second, sem):
        fetch = pltpu.make_async_copy(left_ref.at[pl.ds(cut, rows - cut), :], second, sem)
        fetch.start()
        core = lax.axis_index("k")
        low = lax.broadcasted_iota(jnp.int32, (SET, LANES), 1) < PART
        for y in range(4):
            held = [
                parts_ref[y, jnp.abs(core - k)].astype(F32) + parts_ref[4 + y, jnp.abs(core - k)].astype(F32)
                for k in range(2)
            ]
            for m in range(MB):
                start = m // 2 * LANES
                both = [held[k][:, start : start + LANES] for k in range(2)]
                turned = 1 - m % 2
                both[turned] = pltpu.roll(both[turned], PART, 1)
                whole = jnp.where(low, both[0], both[1])
                at = (m * 4 + y) * LANES
                for f in range(2):
                    scaled[f * SET : (f + 1) * SET, at : at + LANES] = (
                        whole * weights_ref[f : f + 1, at : at + LANES]
                    ).astype(BF16)
        for left, start, stop in ((first_ref, 0, cut), (second, cut, rows)):
            if start == cut:
                fetch.wait()
            product = lax.dot_general(
                scaled[...], left[...], (((1,), (1,)), ((), ())), preferred_element_type=F32
            )
            out_ref[0, :, start:stop] = product[:SET]
            out_ref[1, :, start:stop] = product[SET:]

    return pl.pallas_call(
        kernel,
        out_shape=jax.ShapeDtypeStruct((2, SET, rows), F32),
        in_specs=[VMEM, VMEM, HBM, VMEM],
        out_specs=VMEM,
        scratch_shapes=[
            pltpu.VMEM((2 * SET, NPAIR), BF16),
            pltpu.VMEM((rows - cut, NPAIR), BF16),
            pltpu.SemaphoreType.DMA,
        ],
        compiler_params=pltpu.CompilerParams(vmem_limit_bytes=12 << 20),
        name="screened_response",
    )(parts, first, left_panel, weights)


def shards(
    tiles, tile_blocks, tile_pairs, tile_counts, left_panel, gaps, times, cos_weights, bank, probe_idx
):
    stay = lambda array: pltpu.with_memory_space_constraint(array, pltpu.HBM)
    tiles, tile_blocks, tile_pairs, left_panel = map(stay, (tiles, tile_blocks.reshape(SLOTS), tile_pairs, left_panel))
    swap = [(0, 1), (1, 0)]
    with jax.named_scope("parts"):
        owned = [(f * 8 + z, f * 8 + (z + 4 * f - 2) % 8) for f in range(2) for z in range(8)]
        bank = lax.ppermute(bank, ("f", "z"), owned)
        parts = outgoing_parts(tiles, tile_blocks, tile_pairs, tile_counts)
        parts = lax.all_to_all(after(parts, bank), ("k", "u", "z"), 0, 0, tiled=True, axis_index_groups=runs())
    with jax.named_scope("probes"):
        own = [bank] + [lax.ppermute(bank, "y", [(y, (y + n) % 4) for y in range(4)]) for n in (1, 2, 3)]
        other = [lax.ppermute(columns, "k", swap) for columns in own]
        probes, weights, first = picked_probes(
            own, other, probe_idx.reshape(1, NPROBE), gaps.reshape(1, NPAIR), times, cos_weights, left_panel
        )
    with jax.named_scope("products"):
        products = owner_products(parts, probes)
        products = lax.all_to_all(products, ("u", "z"), 0, 0, tiled=True)
        product = jnp.sum(products.astype(F32), axis=0).astype(BF16)
    with jax.named_scope("spread"):
        both = jnp.stack([product, lax.ppermute(product, "k", swap)])
        both = lax.all_to_all(jnp.broadcast_to(both, (8,) + both.shape), ("f", "y"), 0, 0, tiled=True)
    with jax.named_scope("response"):
        turned = screened_response(both, first, left_panel, weights)
        return jnp.swapaxes(turned, 1, 2)


def solution(mesh):
    fine = Mesh(mesh.devices.reshape(2, 4, 2, 2, 8), ("f", "y", "k", "u", "z"))
    row, col = ("y", "k"), ("u", "z")
    placed = (
        P(col, None, None),
        P(col, None),
        P(col),
        P(col),
        P(row, None),
        P(),
        P(),
        P(),
        P(col, row),
        P(),
    )
    return jax.shard_map(
        shards, mesh=fine, in_specs=placed, out_specs=P("f", row, col), check_vma=False
    )
```
